32 devices in a mesh: rep: 8 (over z, x), tp: 4 (over y, core).
Axes of the slice: x: 2, y: 2, z: 4, core: 2. Of those that a mesh axis runs over, the one named last changes fastest.
Arguments:
- hidden_in: bfloat16 [256, 3584], P('rep'), may hold values from -6 to 6
- k_cache: bfloat16 [256, 4, 64, 128], P('rep', 'tp'), may hold values from -300 to 300, as said below
- v_cache: bfloat16 [256, 4, 64, 128], P('rep', 'tp'), may hold values from -6 to 6
- lengths: int32 [256], replicated, may hold values from 1 to 127, 16384 in all
- routes: int32 [256, 1], replicated, may hold values from 0 to 7; in each aligned block of 32 rows (0 to 31, 32 to 63, ...) at most 8 rows name the same one
- w_query: bfloat16 [3584, 1024], P(None, 'tp'), may hold values from -0.09375 to 0.09375
- b_query: bfloat16 [1024], P('tp'), may hold values from -3 to 3
- w_key: bfloat16 [3584, 256], P(None, 'tp'), may hold values from -0.09375 to 0.09375
- b_key: bfloat16 [256], P('tp'), may hold values from -3 to 3
- w_value: bfloat16 [3584, 256], P(None, 'tp'), may hold values from -0.09375 to 0.09375
- b_value: bfloat16 [256], P('tp'), may hold values from -3 to 3
- w_out: bfloat16 [1024, 3584], P('tp'), may hold values from -0.1875 to 0.1875
- gain_in: bfloat16 [3584], replicated, may hold values from 0.25 to 1.75
- gain_out: bfloat16 [3584], replicated, may hold values from 0.25 to 1.75
- w_head: bfloat16 [19008, 3584], P(('rep', 'tp')), may hold values from -0.09375 to 0.09375
Outputs:
- final_norm: float32 [512], P(('rep', 'tp'))
- top_logit: float32 [512], P(('rep', 'tp'))
- k_cache_out: bfloat16 [512, 4, 64, 128], P('rep', 'tp')
- v_cache_out: bfloat16 [512, 4, 64, 128], P('rep', 'tp')
The draws below stay inside these ranges and needn't reach their ends.
Inputs may be any that keep to these rules, and one draw needn't show every extreme that they name: `routes`: within the 32 requests of one replica at most 8 name the same replica, and in every draw some replica is named exactly 8 times by some replica's requests. `k_cache`: keys are already rotated to their positions.
All inputs are finite; a program needn't handle non-finite values.
Results may differ from the reference program's by a relative error of at most 0.0022.
Values may be sent and summed in bfloat16 or wider, within the bound.
A program may use at most 128 MiB of HBM per device.

```python
import math
import jax
import jax.numpy as jnp
import numpy as np
from jax import lax

D = 3584
HD = 128
V_DEV = 594
SLOTS = 32
MAXLEN = 128
HEADS = 8
KVH = 2
HALF = 64
CAP = 8
SERVE = 64
REQS = 256
VOCAB = 19008
N_REP = 8
N_TP = 4
DEVICES = 32


def draw_k_cache(key, part):
    base = jnp.clip(jax.random.normal(key, (REQS, N_TP, HALF, HD), jnp.float32), -6.0, 6.0)
    return base.astype(jnp.bfloat16)


def block_scale(own_key, shape, cuts, low, top_value):
    gain, own = 1.0, jax.random.fold_in(own_key, 6)
    for axis_at, shards_of in cuts:
        draws = jnp.exp(jax.random.uniform(jax.random.fold_in(own, axis_at), (shards_of,), jnp.float32, low / len(cuts), top_value / len(cuts)))
        gain = gain * jnp.repeat(draws, shape[axis_at] // shards_of).reshape([-1 if axis == axis_at else 1 for axis in range(len(shape))])
    return gain


def profile(number_of, total, most, slope):
    weights = [(1 << 20) // math.isqrt(grade ** slope) + 1 for grade in range(2, number_of + 1)]
    spare, counts = total - most - (number_of - 1), [1] * (number_of - 1)
    while spare > 0:
        candidates = [i for i in range(number_of - 1) if counts[i] < most]
        whole, remaining = sum([weights[i] for i in candidates]), spare
        for i in candidates:
            more = min(most - counts[i], max(1, remaining * weights[i] // whole), spare)
            counts[i] = counts[i] + more
            spare = spare - more
    return np.array([most] + counts)


def uneven_parts(stream_key, amount, total, reach, slope):
    if amount == 2:
        one = jax.random.randint(stream_key, (), max(1, total - reach), min(reach, total - 1) + 1)
        return jnp.stack([one, total - one])
    tallies = jnp.asarray(profile(amount, total, reach, slope), jnp.int32)
    couples = (amount - 1) // 2
    source_of, sink = tallies[1:1 + 2 * couples:2], tallies[2:2 + 2 * couples:2]
    slack = jnp.minimum(source_of - 1, reach - sink)
    moved = jax.random.randint(jax.random.fold_in(stream_key, 1), (couples,), 0, 1 << 20) % (slack + 1)
    tallies = tallies.at[1:1 + 2 * couples:2].set(source_of - moved).at[2:2 + 2 * couples:2].set(sink + moved)
    return tallies[jax.random.permutation(jax.random.fold_in(stream_key, 2), amount)]


def assign_block(stream_key, own, number, rows, number_of, top, most, slope):
    sequence = jax.random.permutation(stream_key, number_of)
    packed, ordinary = shares(number_of, rows * top, most, slope, True), shares(number_of, rows * top, most, slope, False)
    places = jnp.arange(number_of)

    def named(sizes, offset_by):
        used = int((sizes > 0).sum())
        fixed = max(1, used // 4)
        passed = fixed + (places - fixed + offset_by * (used - fixed)) % max(1, number_of - fixed)
        return jnp.zeros((number_of,), jnp.int32).at[sequence[jnp.where(places < fixed, places, passed)]].set(jnp.asarray(sizes, jnp.int32))

    sizes = jnp.where(number % 4 == 0, named(packed, number // 4), named(ordinary, number - number // 4 - 1))
    mixed = jax.random.permutation(jax.random.fold_in(own, 3), number_of)
    source_of, taker = mixed[0:number_of // 2 * 2:2], mixed[1:number_of // 2 * 2:2]
    slack = jnp.minimum(sizes[source_of] - 1, most - sizes[taker]) // 2
    slack = jnp.where((source_of == sequence[0]) | (taker == sequence[0]) | (sizes[taker] == 0), 0, jnp.maximum(slack, 0))
    passed = jax.random.randint(jax.random.fold_in(own, 4), (number_of // 2,), 0, 1 << 20) % (slack + 1)
    sizes = sizes.at[source_of].add(-passed).at[taker].add(passed)
    members = jnp.searchsorted(jnp.cumsum(sizes), jnp.arange(rows * top), side="right").astype(jnp.int32)
    grid = members.reshape(top, rows).T
    grid = grid[jax.random.permutation(jax.random.fold_in(own, 1), rows)]
    offset_by = jax.random.randint(jax.random.fold_in(own, 2), (rows, 1), 0, top)
    return jnp.take_along_axis(grid, (jnp.arange(top)[None, :] + offset_by) % top, axis=1)


def shares(count, total, limit, slope, full):
    weights = [(1 << 20) // math.isqrt(rank ** slope) + 1 for rank in range(1, count + 1)]
    largest = limit if full else min(limit, max(-(-total // count), total * weights[0] // sum(weights)))
    least = 1 if total - largest >= count - 1 else 0
    counts, rest = [largest] + [least] * (count - 1), total - largest - least * (count - 1)
    while rest > 0:
        movable = [i for i in range(1, count) if counts[i] < largest] or [i for i in range(1, count) if counts[i] < limit]
        whole, left = sum([weights[i] for i in movable]), rest
        for i in movable:
            more = min(limit - counts[i], max(1, left * weights[i] // whole), rest)
            counts[i] = counts[i] + more
            rest = rest - more
    return np.array(counts)


def bell_draw(stream_key, extent, width, reach, pieces=(), kind=jnp.bfloat16):
    drawn = width * jax.random.normal(stream_key, extent, jnp.float32)
    if pieces:
        drawn = drawn * block_scale(stream_key, extent, pieces, -0.22, 0.18)
    return jnp.clip(drawn, -reach, reach).astype(kind)


def setup_inputs(seed: int = 0) -> dict:
    seeds = jax.random.split(jax.random.key(seed), 16)
    hidden_in = bell_draw(seeds[0], (REQS, D), 1.0, 6.0, ((0, 8),))
    k_cache = draw_k_cache(jax.random.fold_in(seeds[15], 71), 0)
    v_cache = bell_draw(seeds[2], (REQS, N_TP, HALF, HD), 1.0, 6.0, ((0, 8), (1, 4)))
    lengths = uneven_parts(seeds[3], REQS, REQS * MAXLEN // 2, MAXLEN - 1, 2).astype(jnp.int32)
    routes_keys = jax.random.split(jax.random.fold_in(seeds[4], 1), REQS // SLOTS)
    routes_turns = jax.random.permutation(jax.random.fold_in(seeds[4], 3), REQS // SLOTS)
    routes = jax.vmap(lambda own, number: assign_block(jax.random.fold_in(seeds[4], 2), own, number, SLOTS, N_REP, 1, CAP, 2))(routes_keys, routes_turns).reshape((REQS, 1))
    w_query = bell_draw(seeds[5], (D, HEADS * HD), D ** -0.5, 0.09375, ((1, 4),))
    b_query = bell_draw(seeds[6], (HEADS * HD,), 0.5, 3.0, ((0, 4),))
    w_key = bell_draw(seeds[7], (D, KVH * HD), D ** -0.5, 0.09375, ((1, 4),))
    b_key = bell_draw(seeds[8], (KVH * HD,), 0.5, 3.0, ((0, 4),))
    w_value = bell_draw(seeds[9], (D, KVH * HD), D ** -0.5, 0.09375, ((1, 4),))
    b_value = bell_draw(seeds[10], (KVH * HD,), 0.5, 3.0, ((0, 4),))
    w_out = bell_draw(seeds[11], (HEADS * HD, D), (HEADS * HD) ** -0.5, 0.1875, ((0, 4),))
    gain_in = jnp.clip(1.0 + 0.15 * jax.random.normal(seeds[12], (D,), jnp.float32), 0.25, 1.75).astype(jnp.bfloat16)
    gain_out = jnp.clip(1.0 + 0.15 * jax.random.normal(seeds[13], (D,), jnp.float32), 0.25, 1.75).astype(jnp.bfloat16)
    w_head = bell_draw(seeds[14], (VOCAB, D), D ** -0.5, 0.09375, ((0, 32),))
    return {"hidden_in": hidden_in, "k_cache": k_cache, "v_cache": v_cache, "lengths": lengths, "routes": routes, "w_query": w_query, "b_query": b_query, "w_key": w_key, "b_key": b_key, "w_value": w_value, "b_value": b_value, "w_out": w_out, "gain_in": gain_in, "gain_out": gain_out, "w_head": w_head}


def rotate(vals, positions):
    half = vals.shape[-1] // 2
    freq = 1000000.0 ** (-(jnp.arange(half, dtype=jnp.float32) * 2.0 / vals.shape[-1]))
    angle = positions[..., None] * freq
    first = vals[..., :half]
    second = vals[..., half:]
    return jnp.concatenate([first * jnp.cos(angle) - second * jnp.sin(angle), second * jnp.cos(angle) + first * jnp.sin(angle)], axis=-1)

def destinations(routes):
    flat = routes[:, 0].reshape(N_REP, SLOTS)
    onehot = (flat[:, :, None] == jnp.arange(N_REP, dtype=jnp.int32)[None, None, :]).astype(jnp.int32)
    rank = lax.optimization_barrier(jnp.sum((jnp.cumsum(onehot, axis=1) - onehot) * onehot, axis=2))
    source = jnp.arange(N_REP, dtype=jnp.int32)[:, None]
    return (flat * SERVE + source * CAP + rank).reshape(-1).astype(jnp.int32)

def one_request(args):
    queries, keys, values, key_new, value_new, length = args
    scale = 1.0 / HD ** 0.5
    scores = jnp.einsum('kgd,kpd->kgp', queries.astype(jnp.float32), keys.astype(jnp.float32), precision=lax.Precision.HIGHEST) * scale
    live = (jnp.arange(MAXLEN, dtype=jnp.int32) < length)[None, None, :]
    scores = jnp.where(live, scores, -1e+30)
    own = jnp.einsum('kgd,kd->kg', queries.astype(jnp.float32), key_new.astype(jnp.float32), precision=lax.Precision.HIGHEST) * scale
    peak = jnp.maximum(lax.optimization_barrier(jnp.max(scores, axis=2)), own)
    weights = jnp.where(live, jnp.exp(scores - peak[..., None]), 0.0)
    own_weight = jnp.exp(own - peak)
    total = lax.optimization_barrier(jnp.sum(weights, axis=2)) + own_weight
    mixed = jnp.einsum('kgp,kpd->kgd', weights, values.astype(jnp.float32), precision=lax.Precision.HIGHEST)
    mixed = mixed + own_weight[..., None] * value_new.astype(jnp.float32)[:, None, :]
    return (mixed / total[..., None]).reshape(-1).astype(jnp.bfloat16)

def reference(hidden_in, k_cache, v_cache, lengths, routes, w_query, b_query, w_key, b_key, w_value, b_value, w_out, gain_in, gain_out, w_head):
    eps = 1e-06
    xf = hidden_in.astype(jnp.float32)
    normed_in = (xf * lax.rsqrt(lax.optimization_barrier(jnp.mean(xf * xf, axis=1, keepdims=True)) + eps) * gain_in.astype(jnp.float32)).astype(jnp.bfloat16)
    positions = lengths.astype(jnp.float32)[:, None]
    query = (jnp.dot(normed_in, w_query, preferred_element_type=jnp.float32) + b_query.astype(jnp.float32)).reshape(REQS, HEADS, HD)
    query = rotate(query, positions).astype(jnp.bfloat16)
    key_raw = (jnp.dot(normed_in, w_key, preferred_element_type=jnp.float32) + b_key.astype(jnp.float32)).astype(jnp.bfloat16).reshape(REQS, KVH, HD)
    key_new = rotate(key_raw.astype(jnp.float32), positions).astype(jnp.bfloat16)
    value_new = (jnp.dot(normed_in, w_value, preferred_element_type=jnp.float32) + b_value.astype(jnp.float32)).astype(jnp.bfloat16).reshape(REQS, KVH, HD)
    keys = k_cache.reshape(REQS, KVH, MAXLEN, HD)
    values = v_cache.reshape(REQS, KVH, MAXLEN, HD)
    grouped = query.reshape(REQS, KVH, HEADS // KVH, HD)
    attn = lax.map(one_request, (grouped, keys, values, key_new, value_new, lengths))
    state = (xf + jnp.dot(attn, w_out, preferred_element_type=jnp.float32)).astype(jnp.bfloat16)
    sf = state.astype(jnp.float32)
    ms = lax.optimization_barrier(jnp.mean(sf * sf, axis=1))
    rms = jnp.sqrt(ms)
    normed = (sf * lax.rsqrt(ms + eps)[:, None] * gain_out.astype(jnp.float32)).astype(jnp.bfloat16)
    blocks = w_head.reshape(DEVICES, V_DEV, D)

    def step(best, block):
        logits = lax.dot_general(normed, block, (((1,), (1,)), ((), ())), preferred_element_type=jnp.float32)
        return (jnp.maximum(best, lax.optimization_barrier(jnp.max(logits, axis=1))), None)
    best, _ = lax.scan(step, jnp.full((REQS,), -jnp.inf, jnp.float32), blocks)
    dest = destinations(routes)
    written = (jnp.arange(MAXLEN, dtype=jnp.int32)[None, :] == lengths[:, None])[:, None, :, None]
    keys_full = jnp.where(written, key_new[:, :, None, :], keys).reshape(REQS, N_TP, HALF, HD)
    values_full = jnp.where(written, value_new[:, :, None, :], values).reshape(REQS, N_TP, HALF, HD)
    k_cache_out = jnp.zeros((N_REP * SERVE, N_TP, HALF, HD), jnp.bfloat16).at[dest].set(keys_full)
    v_cache_out = jnp.zeros((N_REP * SERVE, N_TP, HALF, HD), jnp.bfloat16).at[dest].set(values_full)
    final_norm = jnp.zeros((N_REP * SERVE,), jnp.float32).at[dest].set(rms)
    top_logit = jnp.zeros((N_REP * SERVE,), jnp.float32).at[dest].set(best)
    return (final_norm, top_logit, k_cache_out, v_cache_out)
```

```python
import jax
import jax.numpy as jnp
from jax import lax
from jax.sharding import PartitionSpec as P


def swapped(shard, axis, distance):
    return lax.ppermute(shard, axis, [(i, i ^ 1 << distance) for i in range(lax.axis_size(axis))])


def rotate(vals, positions):
    half = vals.shape[-1] // 2
    freq = 1000000.0 ** (-(jnp.arange(half, dtype=jnp.float32) * 2.0 / vals.shape[-1]))
    angle = positions[..., None] * freq
    first = vals[..., :half]
    second = vals[..., half:]
    return jnp.concatenate(
        [
            first * jnp.cos(angle) - second * jnp.sin(angle),
            second * jnp.cos(angle) + first * jnp.sin(angle),
        ],
        axis=-1,
    )


def destinations(routes, n_rep, slots, cap, serve):
    flat = routes[:, 0].reshape(n_rep, slots)
    onehot = (flat[:, :, None] == jnp.arange(n_rep, dtype=jnp.int32)[None, None, :]).astype(
        jnp.int32
    )
    rank = jnp.sum((jnp.cumsum(onehot, axis=1) - onehot) * onehot, axis=2)
    source = jnp.arange(n_rep, dtype=jnp.int32)[:, None]
    return ((flat * serve + source * cap + rank).reshape(-1), flat * cap + rank)


def find_home(dest_flat, targets):
    equal = dest_flat[None, :] == targets[:, None]
    home = jnp.sum(
        jnp.where(equal, jnp.arange(dest_flat.shape[0], dtype=jnp.int32)[None, :], 0), axis=1
    )
    return (home, jnp.any(equal, axis=1))


def fill_buckets(arrays, own_bucket, serve, slots):
    hits = own_bucket[None, :] == jnp.arange(serve, dtype=jnp.int32)[:, None]
    pick = jnp.sum(jnp.where(hits, jnp.arange(slots, dtype=jnp.int32)[None, :], 0), axis=1)
    filled = jnp.any(hits, axis=1)
    return tuple(
        [
            jnp.where(
                filled.reshape((-1,) + (1,) * (item.ndim - 1)),
                item[pick],
                jnp.zeros((), item.dtype),
            )
            for item in arrays
        ]
    )


def write_newest(stored, newest, lens, live_rows, part):
    half_len = stored.shape[1]
    where_pos = part * half_len + jnp.arange(half_len, dtype=jnp.int32)
    written = (where_pos[None, :] == lens[:, None]) & live_rows[:, None]
    return jnp.where(written[:, :, None], newest[:, None, :], stored)


def layer(
    xs,
    keys,
    values,
    lens,
    w_query,
    b_query,
    w_key,
    b_key,
    w_value,
    b_value,
    w_out,
    gain_in,
    gain_out,
    tp_pos,
    n_tp,
):
    eps = 1e-06
    count = xs.shape[0]
    head_size = keys.shape[-1]
    half_len = keys.shape[1]
    part = tp_pos % 2
    even = part == 0
    xf = xs.astype(jnp.float32)
    normed_in = (
        xf * lax.rsqrt(jnp.mean(xf * xf, axis=1, keepdims=True) + eps) * gain_in.astype(jnp.float32)
    ).astype(jnp.bfloat16)
    positions = lens.astype(jnp.float32)[:, None]
    query = (
        jnp.dot(normed_in, w_query, preferred_element_type=jnp.float32)
        + b_query.astype(jnp.float32)
    ).reshape(count, -1, head_size)
    query = rotate(query, positions).astype(jnp.bfloat16)
    key_part = (
        jnp.dot(normed_in, w_key, preferred_element_type=jnp.float32) + b_key.astype(jnp.float32)
    ).astype(jnp.bfloat16)
    value_part = (
        jnp.dot(normed_in, w_value, preferred_element_type=jnp.float32)
        + b_value.astype(jnp.float32)
    ).astype(jnp.bfloat16)
    other_query, other_key, other_value = swapped((query, key_part, value_part), "tp", 0)
    queries = jnp.where(
        even,
        jnp.concatenate([query, other_query], axis=1),
        jnp.concatenate([other_query, query], axis=1),
    )
    key_raw = jnp.where(
        even,
        jnp.concatenate([key_part, other_key], axis=1),
        jnp.concatenate([other_key, key_part], axis=1),
    )
    value_new = jnp.where(
        even,
        jnp.concatenate([value_part, other_value], axis=1),
        jnp.concatenate([other_value, value_part], axis=1),
    )
    key_new = rotate(key_raw.astype(jnp.float32)[:, None, :], positions)[:, 0].astype(jnp.bfloat16)
    scale = 1.0 / head_size**0.5
    scores = jnp.einsum("sgd,spd->sgp", queries, keys, preferred_element_type=jnp.float32) * scale
    place = part * half_len + jnp.arange(half_len, dtype=jnp.int32)
    live = (place[None, :] < lens[:, None])[:, None, :]
    scores = jnp.where(live, scores, -1e30)
    own_score = (
        jnp.einsum("sgd,sd->sg", queries, key_new, preferred_element_type=jnp.float32) * scale
    )
    own_score = jnp.where(even, own_score, -1e30)
    peak = jnp.maximum(jnp.max(scores, axis=2), own_score)
    weights = jnp.where(live, jnp.exp(scores - peak[..., None]), 0.0)
    own_weight = jnp.where(even, jnp.exp(own_score - peak), 0.0)
    total = jnp.sum(weights, axis=2) + own_weight
    mixed = jnp.einsum(
        "sgp,spd->sgd", weights, values.astype(jnp.float32), precision=lax.Precision.HIGHEST
    )
    mixed = mixed + own_weight[..., None] * value_new.astype(jnp.float32)[:, None, :]
    mixed_keep = jnp.where(even, mixed[:, :2], mixed[:, 2:])
    mixed_give = jnp.where(even, mixed[:, 2:], mixed[:, :2])
    peak_keep = jnp.where(even, peak[:, :2], peak[:, 2:])
    peak_give = jnp.where(even, peak[:, 2:], peak[:, :2])
    total_keep = jnp.where(even, total[:, :2], total[:, 2:])
    total_give = jnp.where(even, total[:, 2:], total[:, :2])
    got_mixed, got_peak, got_total = swapped((mixed_give, peak_give, total_give), "tp", 0)
    upper = jnp.maximum(peak_keep, got_peak)
    mine = jnp.exp(peak_keep - upper)
    theirs = jnp.exp(got_peak - upper)
    merged = (mixed_keep * mine[..., None] + got_mixed * theirs[..., None]) / (
        total_keep * mine + got_total * theirs
    )[..., None]
    attn = merged.reshape(count, -1).astype(jnp.bfloat16)
    rows = count // n_tp
    projected = lax.psum_scatter(
        jnp.dot(attn, w_out, preferred_element_type=jnp.float32),
        "tp",
        scatter_dimension=0,
        tiled=True,
    )
    own_x = lax.dynamic_slice_in_dim(xf, tp_pos * rows, rows, 0)
    state = (own_x + projected).astype(jnp.bfloat16)
    sf = state.astype(jnp.float32)
    ms = jnp.mean(sf * sf, axis=1)
    normed = (sf * lax.rsqrt(ms + eps)[:, None] * gain_out.astype(jnp.float32)).astype(jnp.bfloat16)
    return (normed, jnp.sqrt(ms), rows, key_new, value_new)


def spread(item, axis):
    return lax.all_to_all(item, axis, split_axis=0, concat_axis=0, tiled=True)


def choose_own(row, wanted, dest_flat, like):
    hits = dest_flat[None, :] == wanted[:, None]
    return jnp.sum(jnp.where(hits, row[None, :], 0.0), axis=1).astype(like)


def per_device(
    hidden_in,
    k_cache,
    v_cache,
    lengths,
    routes,
    w_query,
    b_query,
    w_key,
    b_key,
    w_value,
    b_value,
    w_out,
    gain_in,
    gain_out,
    w_head,
):
    n_rep = lax.axis_size("rep")
    n_tp = lax.axis_size("tp")
    rep_pos = lax.axis_index("rep")
    tp_pos = lax.axis_index("tp")
    part = tp_pos % 2
    slots = hidden_in.shape[0]
    cap = max(2, 2 * slots // n_rep)
    serve = n_rep * cap
    dest_flat, bucket_grid = destinations(routes, n_rep, slots, cap, serve)
    own_bucket = lax.dynamic_slice_in_dim(bucket_grid, rep_pos, 1, 0)[0]
    keys_home = k_cache[:, 0]
    values_home = v_cache[:, 0]
    weights_all = (w_query, b_query, w_key, b_key, w_value, b_value, w_out, gain_in, gain_out)
    send_k, send_v = fill_buckets((keys_home, values_home), own_bucket, serve, slots)
    got_k, got_v = spread(send_k, "rep"), spread(send_v, "rep")
    home_lens = lax.dynamic_slice_in_dim(lengths, rep_pos * slots, slots, 0)
    normed, norm_own, rows, key_new, value_new = layer(
        hidden_in, keys_home, values_home, home_lens, *weights_all, tp_pos, n_tp
    )
    (send_new,) = fill_buckets(
        (jnp.concatenate([key_new, value_new], axis=1),), own_bucket, serve, slots
    )
    got_new = spread(send_new, "rep")
    head_size = key_new.shape[1]
    targets = rep_pos * serve + jnp.arange(serve, dtype=jnp.int32)
    home, valid = find_home(dest_flat, targets)
    lens = jnp.where(valid, lengths[home], 0)
    keys_served = write_newest(got_k, got_new[:, :head_size], lens, valid, part)
    values_served = write_newest(got_v, got_new[:, head_size:], lens, valid, part)
    logits = lax.dot_general(
        w_head,
        lax.all_gather(normed, ("rep", "tp"), axis=0, tiled=True),
        (((1,), (1,)), ((), ())),
        preferred_element_type=jnp.float32,
    )
    norm_all = lax.dynamic_update_slice_in_dim(
        jnp.zeros((n_rep * slots,), jnp.float32),
        norm_own,
        (rep_pos * n_tp + tp_pos) * rows,
        0,
    )
    both = lax.pmax(jnp.stack([jnp.max(logits, axis=0), norm_all]), ("rep", "tp"))
    share = serve // n_tp
    wanted = (rep_pos * n_tp + tp_pos) * share + jnp.arange(share, dtype=jnp.int32)
    final_norm = choose_own(both[1], wanted, dest_flat, jnp.float32)
    top_logit = choose_own(both[0], wanted, dest_flat, jnp.float32)
    return (final_norm, top_logit, keys_served[:, None], values_served[:, None])


def solution(mesh):
    in_specs = (
        P("rep", None),
        P("rep", "tp", None, None),
        P("rep", "tp", None, None),
        P(),
        P(),
        P(None, "tp"),
        P("tp"),
        P(None, "tp"),
        P("tp"),
        P(None, "tp"),
        P("tp"),
        P("tp", None),
        P(),
        P(),
        P(("rep", "tp"), None),
    )
    out_specs = (
        P(("rep", "tp")),
        P(("rep", "tp")),
        P("rep", "tp", None, None),
        P("rep", "tp", None, None),
    )
    return jax.shard_map(
        per_device, mesh=mesh, in_specs=in_specs, out_specs=out_specs, check_vma=False
    )
```

```python
import functools

import jax
import jax.numpy as jnp
from jax import lax
from jax.experimental import pallas as pl
from jax.experimental.pallas import tpu as pltpu
from jax.sharding import PartitionSpec as P


def swapped(shard, axis, distance):
    return lax.ppermute(shard, axis, [(i, i ^ 1 << distance) for i in range(lax.axis_size(axis))])


def rotate(vals, positions):
    half = vals.shape[-1] // 2
    freq = 1000000.0 ** (-(jnp.arange(half, dtype=jnp.float32) * 2.0 / vals.shape[-1]))
    angle = positions[..., None] * freq
    first = vals[..., :half]
    second = vals[..., half:]
    return jnp.concatenate(
        [
            first * jnp.cos(angle) - second * jnp.sin(angle),
            second * jnp.cos(angle) + first * jnp.sin(angle),
        ],
        axis=-1,
    )


def destinations(routes, n_rep, slots, cap, serve):
    flat = routes[:, 0].reshape(n_rep, slots)
    onehot = (flat[:, :, None] == jnp.arange(n_rep, dtype=jnp.int32)[None, None, :]).astype(
        jnp.int32
    )
    rank = jnp.sum((jnp.cumsum(onehot, axis=1) - onehot) * onehot, axis=2)
    source = jnp.arange(n_rep, dtype=jnp.int32)[:, None]
    return ((flat * serve + source * cap + rank).reshape(-1), flat * cap + rank)


def find_home(dest_flat, targets):
    equal = dest_flat[None, :] == targets[:, None]
    home = jnp.sum(
        jnp.where(equal, jnp.arange(dest_flat.shape[0], dtype=jnp.int32)[None, :], 0), axis=1
    )
    return (home, jnp.any(equal, axis=1))


def fill_buckets(arrays, own_bucket, serve, slots):
    hits = own_bucket[None, :] == jnp.arange(serve, dtype=jnp.int32)[:, None]
    pick = jnp.sum(jnp.where(hits, jnp.arange(slots, dtype=jnp.int32)[None, :], 0), axis=1)
    filled = jnp.any(hits, axis=1)
    return tuple(
        [
            jnp.where(
                filled.reshape((-1,) + (1,) * (item.ndim - 1)),
                item[pick],
                jnp.zeros((), item.dtype),
            )
            for item in arrays
        ]
    )


def write_newest(stored, newest, lens, live_rows, part):
    half_len = stored.shape[1]
    where_pos = part * half_len + jnp.arange(half_len, dtype=jnp.int32)
    written = (where_pos[None, :] == lens[:, None]) & live_rows[:, None]
    return jnp.where(written[:, :, None], newest[:, None, :], stored)


def layer(
    xs,
    keys,
    values,
    lens,
    w_query,
    b_query,
    w_key,
    b_key,
    w_value,
    b_value,
    w_out,
    gain_in,
    gain_out,
    tp_pos,
    n_tp,
):
    eps = 1e-06
    count = xs.shape[0]
    head_size = keys.shape[-1]
    half_len = keys.shape[1]
    part = tp_pos % 2
    even = part == 0
    xf = xs.astype(jnp.float32)
    normed_in = (
        xf * lax.rsqrt(jnp.mean(xf * xf, axis=1, keepdims=True) + eps) * gain_in.astype(jnp.float32)
    ).astype(jnp.bfloat16)
    positions = lens.astype(jnp.float32)[:, None]
    query = (
        jnp.dot(normed_in, w_query, preferred_element_type=jnp.float32)
        + b_query.astype(jnp.float32)
    ).reshape(count, -1, head_size)
    query = rotate(query, positions).astype(jnp.bfloat16)
    key_part = (
        jnp.dot(normed_in, w_key, preferred_element_type=jnp.float32) + b_key.astype(jnp.float32)
    ).astype(jnp.bfloat16)
    value_part = (
        jnp.dot(normed_in, w_value, preferred_element_type=jnp.float32)
        + b_value.astype(jnp.float32)
    ).astype(jnp.bfloat16)
    other_query, other_key, other_value = swapped((query, key_part, value_part), "tp", 0)
    queries = jnp.where(
        even,
        jnp.concatenate([query, other_query], axis=1),
        jnp.concatenate([other_query, query], axis=1),
    )
    key_raw = jnp.where(
        even,
        jnp.concatenate([key_part, other_key], axis=1),
        jnp.concatenate([other_key, key_part], axis=1),
    )
    value_new = jnp.where(
        even,
        jnp.concatenate([value_part, other_value], axis=1),
        jnp.concatenate([other_value, value_part], axis=1),
    )
    key_new = rotate(key_raw.astype(jnp.float32)[:, None, :], positions)[:, 0].astype(jnp.bfloat16)
    scale = 1.0 / head_size**0.5
    scores = jnp.einsum("sgd,spd->sgp", queries, keys, preferred_element_type=jnp.float32) * scale
    place = part * half_len + jnp.arange(half_len, dtype=jnp.int32)
    live = (place[None, :] < lens[:, None])[:, None, :]
    scores = jnp.where(live, scores, -1e30)
    own_score = (
        jnp.einsum("sgd,sd->sg", queries, key_new, preferred_element_type=jnp.float32) * scale
    )
    own_score = jnp.where(even, own_score, -1e30)
    peak = jnp.maximum(jnp.max(scores, axis=2), own_score)
    weights = jnp.where(live, jnp.exp(scores - peak[..., None]), 0.0)
    own_weight = jnp.where(even, jnp.exp(own_score - peak), 0.0)
    total = jnp.sum(weights, axis=2) + own_weight
    mixed = jnp.einsum(
        "sgp,spd->sgd", weights, values.astype(jnp.float32), precision=lax.Precision.HIGHEST
    )
    mixed = mixed + own_weight[..., None] * value_new.astype(jnp.float32)[:, None, :]
    mixed_keep = jnp.where(even, mixed[:, :2], mixed[:, 2:])
    mixed_give = jnp.where(even, mixed[:, 2:], mixed[:, :2])
    peak_keep = jnp.where(even, peak[:, :2], peak[:, 2:])
    peak_give = jnp.where(even, peak[:, 2:], peak[:, :2])
    total_keep = jnp.where(even, total[:, :2], total[:, 2:])
    total_give = jnp.where(even, total[:, 2:], total[:, :2])
    got_mixed, got_peak, got_total = swapped((mixed_give, peak_give, total_give), "tp", 0)
    upper = jnp.maximum(peak_keep, got_peak)
    mine = jnp.exp(peak_keep - upper)
    theirs = jnp.exp(got_peak - upper)
    merged = (mixed_keep * mine[..., None] + got_mixed * theirs[..., None]) / (
        total_keep * mine + got_total * theirs
    )[..., None]
    attn = merged.reshape(count, -1).astype(jnp.bfloat16)
    rows = count // n_tp
    projected = lax.psum_scatter(
        jnp.dot(attn, w_out, preferred_element_type=jnp.float32),
        "tp",
        scatter_dimension=0,
        tiled=True,
    )
    own_x = lax.dynamic_slice_in_dim(xf, tp_pos * rows, rows, 0)
    state = (own_x + projected).astype(jnp.bfloat16)
    sf = state.astype(jnp.float32)
    ms = jnp.mean(sf * sf, axis=1)
    normed = (sf * lax.rsqrt(ms + eps)[:, None] * gain_out.astype(jnp.float32)).astype(jnp.bfloat16)
    return (normed, jnp.sqrt(ms), rows, key_new, value_new)


def spread(item, axis):
    return lax.all_to_all(item, axis, split_axis=0, concat_axis=0, tiled=True)


def choose_own(row, wanted, dest_flat, like):
    hits = dest_flat[None, :] == wanted[:, None]
    return jnp.sum(jnp.where(hits, row[None, :], 0.0), axis=1).astype(like)


def per_device(
    hidden_in,
    k_cache,
    v_cache,
    lengths,
    routes,
    w_query,
    b_query,
    w_key,
    b_key,
    w_value,
    b_value,
    w_out,
    gain_in,
    gain_out,
    w_head,
):
    n_rep = lax.axis_size("rep")
    n_tp = lax.axis_size("tp")
    rep_pos = lax.axis_index("rep")
    tp_pos = lax.axis_index("tp")
    part = tp_pos % 2
    slots = hidden_in.shape[0]
    cap = max(2, 2 * slots // n_rep)
    serve = n_rep * cap
    dest_flat, bucket_grid = destinations(routes, n_rep, slots, cap, serve)
    own_bucket = lax.dynamic_slice_in_dim(bucket_grid, rep_pos, 1, 0)[0]
    keys_home = k_cache[:, 0]
    values_home = v_cache[:, 0]
    weights_all = (w_query, b_query, w_key, b_key, w_value, b_value, w_out, gain_in, gain_out)
    send_k, send_v = fill_buckets((keys_home, values_home), own_bucket, serve, slots)
    got_k, got_v = spread(send_k, "rep"), spread(send_v, "rep")
    home_lens = lax.dynamic_slice_in_dim(lengths, rep_pos * slots, slots, 0)
    normed, norm_own, rows, key_new, value_new = layer(
        hidden_in, keys_home, values_home, home_lens, *weights_all, tp_pos, n_tp
    )
    (send_new,) = fill_buckets(
        (jnp.concatenate([key_new, value_new], axis=1),), own_bucket, serve, slots
    )
    got_new = spread(send_new, "rep")
    head_size = key_new.shape[1]
    targets = rep_pos * serve + jnp.arange(serve, dtype=jnp.int32)
    home, valid = find_home(dest_flat, targets)
    lens = jnp.where(valid, lengths[home], 0)
    keys_served = write_newest(got_k, got_new[:, :head_size], lens, valid, part)
    values_served = write_newest(got_v, got_new[:, head_size:], lens, valid, part)
    logits = lax.dot_general(
        w_head,
        lax.all_gather(normed, ("rep", "tp"), axis=0, tiled=True),
        (((1,), (1,)), ((), ())),
        preferred_element_type=jnp.float32,
    )
    norm_all = lax.dynamic_update_slice_in_dim(
        jnp.zeros((n_rep * slots,), jnp.float32),
        norm_own,
        (rep_pos * n_tp + tp_pos) * rows,
        0,
    )
    both = lax.pmax(jnp.stack([jnp.max(logits, axis=0), norm_all]), ("rep", "tp"))
    share = serve // n_tp
    wanted = (rep_pos * n_tp + tp_pos) * share + jnp.arange(share, dtype=jnp.int32)
    final_norm = choose_own(both[1], wanted, dest_flat, jnp.float32)
    top_logit = choose_own(both[0], wanted, dest_flat, jnp.float32)
    return (final_norm, top_logit, keys_served[:, None], values_served[:, None])


MESH = pl.DeviceIdType.MESH


def fused(
    n_rep,
    n_tp,
    pick,
    hid,
    cosf,
    sinf,
    lens,
    onehot,
    bq,
    bk,
    bv,
    gin,
    gout,
    k_hbm,
    v_hbm,
    wq_hbm,
    wk_hbm,
    wv_hbm,
    wo_hbm,
    wh_hbm,
    out_k,
    out_v,
    out_new,
    out_max,
    kz,
    vz,
    kb,
    vb,
    wq,
    wk,
    wv,
    wo,
    wh,
    xf_s,
    pair,
    mixed_s,
    mixed_r,
    nb,
    rs_s,
    rs_b,
    rs_r,
    ag,
    xs,
    top_s,
    top_r,
    top2_s,
    top2_r,
    load_sem,
    keep_sem,
    cs,
    cr,
    ns,
    nr,
    ps,
    pr,
    rss,
    rsr,
    ags,
    agr,
    ts,
    tr,
):
    f32, bf16 = jnp.float32, jnp.bfloat16
    eps = 1e-06
    rep = lax.axis_index("rep")
    tp = lax.axis_index("tp")
    z, x = rep // 2, rep % 2
    y, c = tp // 2, tp % 2
    slots, d = hid.shape
    half_len, hd = kz.shape[1:]
    cap = kb.shape[0] // n_rep
    rows = slots // n_tp
    half_d = d // 2
    mate = tp + 1 - 2 * c
    me = rep * n_tp + tp

    def remote(src, dst, send, recv, rep_to, tp_to):
        return pltpu.make_async_remote_copy(
            src_ref=src,
            dst_ref=dst,
            send_sem=send,
            recv_sem=recv,
            device_id=(rep_to, tp_to),
            device_id_type=MESH,
        )

    loads = [
        pltpu.make_async_copy(src, dst, load_sem.at[i])
        for i, (src, dst) in enumerate(
            [
                (k_hbm, kz.at[pl.ds(0, slots)]),
                (v_hbm, vz.at[pl.ds(0, slots)]),
                (wq_hbm, wq),
                (wk_hbm, wk),
                (wv_hbm, wv),
                (wo_hbm, wo),
                (wh_hbm, wh),
            ]
        )
    ]
    for item in loads:
        item.start()
    kz[slots] = jnp.zeros((half_len, hd), bf16)
    vz[slots] = jnp.zeros((half_len, hd), bf16)

    barrier = pltpu.get_barrier_semaphore()
    for s in range(1, n_rep):
        pl.semaphore_signal(
            barrier, inc=1, device_id=((rep + s) % n_rep, tp), device_id_type=MESH
        )
    for s in range(1, n_tp):
        pl.semaphore_signal(
            barrier, inc=1, device_id=(rep, (tp + s) % n_tp), device_id_type=MESH
        )
    pl.semaphore_wait(barrier, n_rep - 1 + n_tp - 1)

    loads[0].wait()
    loads[1].wait()
    sends = []
    own = pl.ds(rep * cap, cap)
    for s in list(range(1, n_rep)) + [0]:
        to = (rep + s) % n_rep
        there = pl.ds(to * cap, cap)
        for which, (src, buf, out) in enumerate(((kz, kb, out_k), (vz, vb, out_v))):

            def fill(j, carry, src=src, buf=buf, to=to):
                buf[to * cap + j] = src[pick[to * cap + j]]
                return carry

            lax.fori_loop(0, cap, fill, 0)
            if s:
                copy = remote(
                    buf.at[there], out.at[own], cs.at[which, s], cr.at[which, s], to, tp
                )
            else:
                copy = pltpu.make_async_copy(buf.at[own], out.at[own], keep_sem.at[which])
            copy.start()
            sends.append((s, which, copy))

    xf = hid[...].astype(f32)
    xf_s[...] = xf
    scale_in = lax.rsqrt(jnp.mean(xf * xf, axis=1, keepdims=True) + eps)
    normed_in = (xf * scale_in * gin[...].astype(f32)).astype(bf16)
    cos, sin = cosf[...], sinf[...]

    def turn(vals):
        return vals * cos + pltpu.roll(vals, hd // 2, 1) * sin

    loads[2].wait()
    query = jnp.dot(normed_in, wq[...], preferred_element_type=f32) + bq[...].astype(f32)
    loads[3].wait()
    key_part = jnp.dot(normed_in, wk[...], preferred_element_type=f32) + bk[...].astype(f32)
    loads[4].wait()
    value_part = jnp.dot(normed_in, wv[...], preferred_element_type=f32) + bv[...].astype(f32)
    pair[c] = jnp.concatenate(
        [
            turn(query[:, :hd]),
            turn(query[:, hd:]),
            jnp.concatenate([key_part, value_part], axis=1),
        ],
        axis=0,
    ).astype(bf16)
    swap = remote(pair.at[c], pair.at[c], ps.at[0], pr.at[0], rep, mate)
    swap.start()

    swap.wait_send()
    remote(pair.at[1 - c], pair.at[1 - c], ps.at[0], pr.at[0], rep, mate).wait_recv()
    first = pair[0].astype(f32)
    second = pair[1].astype(f32)
    queries = jnp.concatenate([first[: 2 * slots], second[: 2 * slots]], axis=0)
    key_raw = jnp.concatenate(
        [first[2 * slots :, : hd // 2], second[2 * slots :, : hd // 2]], axis=1
    )
    value_new = jnp.concatenate(
        [first[2 * slots :, hd // 2 :], second[2 * slots :, hd // 2 :]], axis=1
    )
    key_new = turn(key_raw).astype(bf16).astype(f32)
    new_k = jnp.dot(onehot[...], key_new.astype(bf16), preferred_element_type=f32)
    new_v = jnp.dot(onehot[...], value_new.astype(bf16), preferred_element_type=f32)
    for t in range(n_rep):
        cut = slice(t * cap, (t + 1) * cap)
        nb[t] = jnp.concatenate([new_k[cut], new_v[cut]], axis=0).astype(bf16)
    new_sends = []
    for s in range(1, n_rep):
        to = (rep + s) % n_rep
        copy = remote(nb.at[to], out_new.at[rep], ns.at[s], nr.at[s], to, tp)
        copy.start()
        new_sends.append(copy)
    out_new[rep] = nb[rep]

    count = 4 * slots
    scale = 1.0 / hd**0.5
    keys = kz[0:slots].reshape(slots * half_len, hd)
    values = vz[0:slots].reshape(slots * half_len, hd)
    scores = (
        lax.dot_general(
            queries.astype(bf16), keys, (((1,), (1,)), ((), ())), preferred_element_type=f32
        )
        * scale
    )
    row = lax.broadcasted_iota(jnp.int32, scores.shape, 0)
    col = lax.broadcasted_iota(jnp.int32, scores.shape, 1)
    live = (col // half_len == row % slots) & (col % half_len + c * half_len < lens[...])
    scores = jnp.where(live, scores, -1e30)
    own_score = (
        jnp.sum(queries * jnp.concatenate([key_new] * 4, axis=0), axis=1, keepdims=True) * scale
    )
    even = jnp.broadcast_to(c, (count, 1)) == 0
    own_score = jnp.where(even, own_score, -1e30)
    peak = jnp.maximum(jnp.max(scores, axis=1, keepdims=True), own_score)
    weights = jnp.where(live, jnp.exp(scores - peak), 0.0)
    own_weight = jnp.where(even, jnp.exp(own_score - peak), 0.0)
    total = jnp.sum(weights, axis=1, keepdims=True) + own_weight
    high = weights.astype(bf16)
    low = (weights - high.astype(f32)).astype(bf16)
    mixed = jnp.dot(high, values, preferred_element_type=f32) + jnp.dot(
        low, values, preferred_element_type=f32
    )
    mixed = mixed + own_weight * jnp.concatenate([value_new] * 4, axis=0)
    lane = lax.broadcasted_iota(jnp.int32, (count, hd), 1)
    stats = jnp.where(lane < hd // 2, peak, total)
    both = jnp.concatenate([mixed, stats], axis=1)
    mixed_s[0] = both[: 2 * slots]
    mixed_s[1] = both[2 * slots :]
    swap = remote(mixed_s.at[1 - c], mixed_r, ps.at[1], pr.at[1], rep, mate)
    swap.start()
    swap.wait()
    keep = mixed_s[c]
    got = mixed_r[...]
    peak_keep, total_keep = keep[:, hd : hd + 1], keep[:, 2 * hd - 1 : 2 * hd]
    peak_got, total_got = got[:, hd : hd + 1], got[:, 2 * hd - 1 : 2 * hd]
    upper = jnp.maximum(peak_keep, peak_got)
    mine = jnp.exp(peak_keep - upper)
    theirs = jnp.exp(peak_got - upper)
    merged = (keep[:, :hd] * mine + got[:, :hd] * theirs) / (
        total_keep * mine + total_got * theirs
    )
    attn = jnp.concatenate([merged[:slots], merged[slots:]], axis=1).astype(bf16)

    loads[5].wait()
    projected = jnp.dot(attn, wo[...], preferred_element_type=f32)
    for t in range(n_tp):
        cut = projected[t * rows : (t + 1) * rows]
        rs_s[t] = jnp.concatenate([cut[:, :half_d], cut[:, half_d:]], axis=0)
    for t in range(n_tp):
        rs_b[t] = rs_s[t].astype(bf16)
    rs_sends = []
    for s in range(1, n_tp):
        to = (tp + s) % n_tp
        copy = remote(rs_b.at[to], rs_r.at[s], rss.at[s], rsr.at[s], rep, to)
        copy.start()
        rs_sends.append(copy)
    summed = rs_s[tp]
    for s, copy in enumerate(rs_sends):
        copy.wait()
        summed = summed + rs_r[s + 1].astype(f32)
    own_x = xf_s[pl.ds(tp * rows, rows)]
    state = (
        (own_x + jnp.concatenate([summed[:rows], summed[rows:]], axis=1)).astype(bf16).astype(f32)
    )
    ms = jnp.mean(state * state, axis=1, keepdims=True)
    normed = state * lax.rsqrt(ms + eps) * gout[...].astype(f32)
    ag[me] = jnp.concatenate([normed[:, :half_d], normed[:, half_d:]], axis=0).astype(bf16)

    x1, y1 = 1 - x, 1 - y
    rep_x = rep + 1 - 2 * x
    tp_y = tp + 2 - 4 * y
    rep_first, tp_first = c * rep + (1 - c) * rep_x, (1 - c) * tp + c * tp_y
    rep_second, tp_second = (1 - c) * rep + c * rep_x, c * tp + (1 - c) * tp_y
    x_first, x_second = c * x + (1 - c) * x1, (1 - c) * x + c * x1
    n_z = n_rep // 2
    base_b, base_c, base_d = n_z, 2 * n_z, 4 * n_z
    ag_sends = []

    def push(block, at, rep_to, tp_to):
        copy = remote(ag.at[block], ag.at[block], ags.at[at], agr.at[at], rep_to, tp_to)
        copy.start()
        ag_sends.append(copy)

    def arrived(block, at):
        remote(ag.at[block], ag.at[block], ags.at[at], agr.at[at], rep, mate).wait_recv()

    for s in range(1, n_z):
        push(me, s, ((z + s) % n_z) * 2 + x, tp)
    plane = [(z + n_z - s) % n_z for s in range(n_z)]
    for s in range(n_z):
        block = (plane[s] * 2 + x) * n_tp + tp
        if s:
            arrived(block, s)
        push(block, base_b + s, rep_first, tp_first)
        push(block, base_c + s, rep_second, tp_second)
        push(block, base_d + s, rep, mate)
    for s in range(n_z):
        block = (plane[s] * 2 + x_first) * n_tp + tp_first
        arrived(block, base_b + s)
        push(block, base_c + n_z + s, rep_second, tp_second)
        push(block, base_d + n_z + s, rep, mate)
    for s in range(n_z):
        block = (plane[s] * 2 + x_second) * n_tp + tp_second
        arrived(block, base_c + s)
        push(block, base_d + 2 * n_z + s, rep, mate)
    for s in range(n_z):
        block = (plane[s] * 2 + x1) * n_tp + tp_y
        arrived(block, base_c + n_z + s)
        push(block, base_d + 3 * n_z + s, rep, mate)
    other_y = mate + 2 - 4 * y
    x_first_m, x_second_m = x_second, x_first
    tp_first_m = c * mate + (1 - c) * other_y
    tp_second_m = (1 - c) * mate + c * other_y
    for s in range(n_z):
        arrived((plane[s] * 2 + x) * n_tp + mate, base_d + s)
        arrived((plane[s] * 2 + x_first_m) * n_tp + tp_first_m, base_d + n_z + s)
        arrived((plane[s] * 2 + x_second_m) * n_tp + tp_second_m, base_d + 2 * n_z + s)
        arrived((plane[s] * 2 + x1) * n_tp + other_y, base_d + 3 * n_z + s)
    for copy in ag_sends:
        copy.wait_send()

    reqs = n_rep * slots
    width = 256
    for i in range(half_d // width):
        part = ag[:, :, i * width : (i + 1) * width].astype(f32)
        for h in range(2):
            xs[:, h * half_d + i * width : h * half_d + (i + 1) * width] = (
                part[:, h * rows : (h + 1) * rows].reshape(reqs, width).astype(bf16)
            )
    loads[6].wait()
    vocab = wh.shape[0]
    cuts = list(range(0, vocab, 208)) + [vocab]
    best = None
    for low_at, high_at in zip(cuts[:-1], cuts[1:]):
        logits = lax.dot_general(
            wh[low_at:high_at], xs[...], (((1,), (1,)), ((), ())), preferred_element_type=f32
        )
        one = jnp.max(logits, axis=0, keepdims=True)
        best = one if best is None else jnp.maximum(best, one)
    at_row = lax.broadcasted_iota(jnp.int32, (rows, reqs), 0)
    at_lane = lax.broadcasted_iota(jnp.int32, (rows, reqs), 1)
    rms = jnp.max(
        jnp.where(at_lane == at_row + me * rows, jnp.sqrt(ms), 0.0), axis=0, keepdims=True
    )
    top = jnp.where(at_row == 0, best, rms)
    top_s[...] = top
    hops = []
    for s in range(1, n_rep):
        copy = remote(top_s, top_r.at[s], ts.at[s], tr.at[s], (rep + s) % n_rep, tp)
        copy.start()
        hops.append(copy)
    for s, copy in enumerate(hops):
        copy.wait()
        top = jnp.maximum(top, top_r[s + 1])
    top2_s[...] = top
    hops = []
    for s in range(1, n_tp):
        at = n_rep + s
        copy = remote(top2_s, top2_r.at[s], ts.at[at], tr.at[at], rep, (tp + s) % n_tp)
        copy.start()
        hops.append(copy)
    for s, copy in enumerate(hops):
        copy.wait()
        top = jnp.maximum(top, top2_r[s + 1])
    out_max[...] = top

    for copy in new_sends:
        copy.wait()
    for _, _, copy in sends:
        copy.wait()


def fast_device(
    hidden_in,
    k_cache,
    v_cache,
    lengths,
    routes,
    w_query,
    b_query,
    w_key,
    b_key,
    w_value,
    b_value,
    w_out,
    gain_in,
    gain_out,
    w_head,
):
    n_rep = lax.axis_size("rep")
    n_tp = lax.axis_size("tp")
    rep_pos = lax.axis_index("rep")
    tp_pos = lax.axis_index("tp")
    part = tp_pos % 2
    slots, width = hidden_in.shape
    half_len, hd = k_cache.shape[2:]
    cap = max(2, 2 * slots // n_rep)
    serve = n_rep * cap
    rows = slots // n_tp
    reqs = n_rep * slots
    flat = routes[:, 0].reshape(n_rep, slots)
    order = jnp.arange(slots, dtype=jnp.int32)
    before = (flat[:, :, None] == flat[:, None, :]) & (order[None, None, :] < order[None, :, None])
    rank = jnp.sum(before.astype(jnp.int32), axis=2)
    source = jnp.arange(n_rep, dtype=jnp.int32)[:, None]
    dest_flat = (flat * serve + source * cap + rank).reshape(-1)
    own_bucket = lax.dynamic_slice_in_dim(flat * cap + rank, rep_pos, 1, 0)[0]
    hits = own_bucket[None, :] == jnp.arange(serve, dtype=jnp.int32)[:, None]
    pick = slots + jnp.sum(jnp.where(hits, order[None, :] - slots, 0), axis=1)
    onehot = hits.astype(jnp.bfloat16)
    home_lens = lax.dynamic_slice_in_dim(lengths, rep_pos * slots, slots, 0)
    freq = 1000000.0 ** (-(jnp.arange(hd // 2, dtype=jnp.float32) * 2.0 / hd))
    angle = home_lens.astype(jnp.float32)[:, None] * freq
    cos, sin = jnp.cos(angle), jnp.sin(angle)
    cosf = jnp.concatenate([cos, cos], axis=1)
    sinf = jnp.concatenate([-sin, sin], axis=1)
    bf16, f32 = jnp.bfloat16, jnp.float32
    vmem = pl.BlockSpec(memory_space=pltpu.VMEM)
    anywhere = pl.BlockSpec(memory_space=pl.ANY)
    dma = pltpu.SemaphoreType.DMA
    block = (2 * rows, width // 2)
    got_k, got_v, got_new, best = pl.pallas_call(
        functools.partial(fused, n_rep, n_tp),
        out_shape=[
            jax.ShapeDtypeStruct((serve, half_len, hd), bf16),
            jax.ShapeDtypeStruct((serve, half_len, hd), bf16),
            jax.ShapeDtypeStruct((n_rep, 2 * cap, hd), bf16),
            jax.ShapeDtypeStruct((8, reqs), f32),
        ],
        in_specs=[pl.BlockSpec(memory_space=pltpu.SMEM)] + [vmem] * 10 + [anywhere] * 7,
        out_specs=[anywhere, anywhere, vmem, vmem],
        scratch_shapes=[
            pltpu.VMEM((slots + 1, half_len, hd), bf16),
            pltpu.VMEM((slots + 1, half_len, hd), bf16),
            pltpu.VMEM((serve, half_len, hd), bf16),
            pltpu.VMEM((serve, half_len, hd), bf16),
            pltpu.VMEM(w_query.shape, bf16),
            pltpu.VMEM(w_key.shape, bf16),
            pltpu.VMEM(w_value.shape, bf16),
            pltpu.VMEM(w_out.shape, bf16),
            pltpu.VMEM(w_head.shape, bf16),
            pltpu.VMEM((slots, width), f32),
            pltpu.VMEM((2, 3 * slots, hd), bf16),
            pltpu.VMEM((2, 2 * slots, 2 * hd), f32),
            pltpu.VMEM((2 * slots, 2 * hd), f32),
            pltpu.VMEM((n_rep, 2 * cap, hd), bf16),
            pltpu.VMEM((n_tp,) + block, f32),
            pltpu.VMEM((n_tp,) + block, bf16),
            pltpu.VMEM((n_tp,) + block, bf16),
            pltpu.VMEM((n_rep * n_tp,) + block, bf16),
            pltpu.VMEM((reqs, width), bf16),
            pltpu.VMEM((8, reqs), f32),
            pltpu.VMEM((n_rep, 8, reqs), f32),
            pltpu.VMEM((8, reqs), f32),
            pltpu.VMEM((n_tp, 8, reqs), f32),
            dma((7,)),
            dma((2,)),
            dma((2, n_rep)),
            dma((2, n_rep)),
            dma((n_rep,)),
            dma((n_rep,)),
            dma((2,)),
            dma((2,)),
            dma((n_tp,)),
            dma((n_tp,)),
            dma((4 * n_rep,)),
            dma((4 * n_rep,)),
            dma((n_rep + n_tp,)),
            dma((n_rep + n_tp,)),
        ],
        compiler_params=pltpu.CompilerParams(
            collective_id=0, has_side_effects=True, vmem_limit_bytes=40 * 1024 * 1024
        ),
    )(
        pick,
        hidden_in,
        cosf,
        sinf,
        jnp.tile(home_lens, 4)[:, None],
        onehot,
        b_query[None],
        b_key[None],
        b_value[None],
        gain_in[None],
        gain_out[None],
        k_cache[:, 0],
        v_cache[:, 0],
        w_query,
        w_key,
        w_value,
        w_out,
        w_head,
    )
    new = got_new.reshape(n_rep, 2, cap, hd)
    new_k = new[:, 0].reshape(serve, hd)
    new_v = new[:, 1].reshape(serve, hd)
    targets = rep_pos * serve + jnp.arange(serve, dtype=jnp.int32)
    equal = dest_flat[None, :] == targets[:, None]
    lens = jnp.sum(jnp.where(equal, lengths[None, :] + 1, 0), axis=1) - 1
    valid = lens >= 0
    keys_served = write_newest(got_k, new_k, lens, valid, part)
    values_served = write_newest(got_v, new_v, lens, valid, part)
    share = serve // n_tp
    wanted = (rep_pos * n_tp + tp_pos) * share + jnp.arange(share, dtype=jnp.int32)
    final_norm = choose_own(best[1], wanted, dest_flat, f32)
    top_logit = choose_own(best[0], wanted, dest_flat, f32)
    return (final_norm, top_logit, keys_served[:, None], values_served[:, None])


def solution(mesh):
    in_specs = (
        P("rep", None),
        P("rep", "tp", None, None),
        P("rep", "tp", None, None),
        P(),
        P(),
        P(None, "tp"),
        P("tp"),
        P(None, "tp"),
        P("tp"),
        P(None, "tp"),
        P("tp"),
        P("tp", None),
        P(),
        P(),
        P(("rep", "tp"), None),
    )
    out_specs = (
        P(("rep", "tp")),
        P(("rep", "tp")),
        P("rep", "tp", None, None),
        P("rep", "tp", None, None),
    )
    small = mesh.shape["rep"] == 8 and mesh.shape["tp"] == 4
    return jax.shard_map(
        fast_device if small else per_device, mesh=mesh, in_specs=in_specs, out_specs=out_specs, check_vma=False
    )
```

```python
import functools

import jax
import jax.numpy as jnp
from jax import lax
from jax.experimental import pallas as pl
from jax.experimental.pallas import tpu as pltpu
from jax.sharding import PartitionSpec as P


def swapped(shard, axis, distance):
    return lax.ppermute(shard, axis, [(i, i ^ 1 << distance) for i in range(lax.axis_size(axis))])


def rotate(vals, positions):
    half = vals.shape[-1] // 2
    freq = 1000000.0 ** (-(jnp.arange(half, dtype=jnp.float32) * 2.0 / vals.shape[-1]))
    angle = positions[..., None] * freq
    first = vals[..., :half]
    second = vals[..., half:]
    return jnp.concatenate(
        [
            first * jnp.cos(angle) - second * jnp.sin(angle),
            second * jnp.cos(angle) + first * jnp.sin(angle),
        ],
        axis=-1,
    )


def destinations(routes, n_rep, slots, cap, serve):
    flat = routes[:, 0].reshape(n_rep, slots)
    onehot = (flat[:, :, None] == jnp.arange(n_rep, dtype=jnp.int32)[None, None, :]).astype(
        jnp.int32
    )
    rank = jnp.sum((jnp.cumsum(onehot, axis=1) - onehot) * onehot, axis=2)
    source = jnp.arange(n_rep, dtype=jnp.int32)[:, None]
    return ((flat * serve + source * cap + rank).reshape(-1), flat * cap + rank)


def find_home(dest_flat, targets):
    equal = dest_flat[None, :] == targets[:, None]
    home = jnp.sum(
        jnp.where(equal, jnp.arange(dest_flat.shape[0], dtype=jnp.int32)[None, :], 0), axis=1
    )
    return (home, jnp.any(equal, axis=1))


def fill_buckets(arrays, own_bucket, serve, slots):
    hits = own_bucket[None, :] == jnp.arange(serve, dtype=jnp.int32)[:, None]
    pick = jnp.sum(jnp.where(hits, jnp.arange(slots, dtype=jnp.int32)[None, :], 0), axis=1)
    filled = jnp.any(hits, axis=1)
    return tuple(
        [
            jnp.where(
                filled.reshape((-1,) + (1,) * (item.ndim - 1)),
                item[pick],
                jnp.zeros((), item.dtype),
            )
            for item in arrays
        ]
    )


def write_newest(stored, newest, lens, live_rows, part):
    half_len = stored.shape[1]
    where_pos = part * half_len + jnp.arange(half_len, dtype=jnp.int32)
    written = (where_pos[None, :] == lens[:, None]) & live_rows[:, None]
    return jnp.where(written[:, :, None], newest[:, None, :], stored)


def layer(
    xs,
    keys,
    values,
    lens,
    w_query,
    b_query,
    w_key,
    b_key,
    w_value,
    b_value,
    w_out,
    gain_in,
    gain_out,
    tp_pos,
    n_tp,
):
    eps = 1e-06
    count = xs.shape[0]
    head_size = keys.shape[-1]
    half_len = keys.shape[1]
    part = tp_pos % 2
    even = part == 0
    xf = xs.astype(jnp.float32)
    normed_in = (
        xf * lax.rsqrt(jnp.mean(xf * xf, axis=1, keepdims=True) + eps) * gain_in.astype(jnp.float32)
    ).astype(jnp.bfloat16)
    positions = lens.astype(jnp.float32)[:, None]
    query = (
        jnp.dot(normed_in, w_query, preferred_element_type=jnp.float32)
        + b_query.astype(jnp.float32)
    ).reshape(count, -1, head_size)
    query = rotate(query, positions).astype(jnp.bfloat16)
    key_part = (
        jnp.dot(normed_in, w_key, preferred_element_type=jnp.float32) + b_key.astype(jnp.float32)
    ).astype(jnp.bfloat16)
    value_part = (
        jnp.dot(normed_in, w_value, preferred_element_type=jnp.float32)
        + b_value.astype(jnp.float32)
    ).astype(jnp.bfloat16)
    other_query, other_key, other_value = swapped((query, key_part, value_part), "tp", 0)
    queries = jnp.where(
        even,
        jnp.concatenate([query, other_query], axis=1),
        jnp.concatenate([other_query, query], axis=1),
    )
    key_raw = jnp.where(
        even,
        jnp.concatenate([key_part, other_key], axis=1),
        jnp.concatenate([other_key, key_part], axis=1),
    )
    value_new = jnp.where(
        even,
        jnp.concatenate([value_part, other_value], axis=1),
        jnp.concatenate([other_value, value_part], axis=1),
    )
    key_new = rotate(key_raw.astype(jnp.float32)[:, None, :], positions)[:, 0].astype(jnp.bfloat16)
    scale = 1.0 / head_size**0.5
    scores = jnp.einsum("sgd,spd->sgp", queries, keys, preferred_element_type=jnp.float32) * scale
    place = part * half_len + jnp.arange(half_len, dtype=jnp.int32)
    live = (place[None, :] < lens[:, None])[:, None, :]
    scores = jnp.where(live, scores, -1e30)
    own_score = (
        jnp.einsum("sgd,sd->sg", queries, key_new, preferred_element_type=jnp.float32) * scale
    )
    own_score = jnp.where(even, own_score, -1e30)
    peak = jnp.maximum(jnp.max(scores, axis=2), own_score)
    weights = jnp.where(live, jnp.exp(scores - peak[..., None]), 0.0)
    own_weight = jnp.where(even, jnp.exp(own_score - peak), 0.0)
    total = jnp.sum(weights, axis=2) + own_weight
    mixed = jnp.einsum(
        "sgp,spd->sgd", weights, values.astype(jnp.float32), precision=lax.Precision.HIGHEST
    )
    mixed = mixed + own_weight[..., None] * value_new.astype(jnp.float32)[:, None, :]
    mixed_keep = jnp.where(even, mixed[:, :2], mixed[:, 2:])
    mixed_give = jnp.where(even, mixed[:, 2:], mixed[:, :2])
    peak_keep = jnp.where(even, peak[:, :2], peak[:, 2:])
    peak_give = jnp.where(even, peak[:, 2:], peak[:, :2])
    total_keep = jnp.where(even, total[:, :2], total[:, 2:])
    total_give = jnp.where(even, total[:, 2:], total[:, :2])
    got_mixed, got_peak, got_total = swapped((mixed_give, peak_give, total_give), "tp", 0)
    upper = jnp.maximum(peak_keep, got_peak)
    mine = jnp.exp(peak_keep - upper)
    theirs = jnp.exp(got_peak - upper)
    merged = (mixed_keep * mine[..., None] + got_mixed * theirs[..., None]) / (
        total_keep * mine + got_total * theirs
    )[..., None]
    attn = merged.reshape(count, -1).astype(jnp.bfloat16)
    rows = count // n_tp
    projected = lax.psum_scatter(
        jnp.dot(attn, w_out, preferred_element_type=jnp.float32),
        "tp",
        scatter_dimension=0,
        tiled=True,
    )
    own_x = lax.dynamic_slice_in_dim(xf, tp_pos * rows, rows, 0)
    state = (own_x + projected).astype(jnp.bfloat16)
    sf = state.astype(jnp.float32)
    ms = jnp.mean(sf * sf, axis=1)
    normed = (sf * lax.rsqrt(ms + eps)[:, None] * gain_out.astype(jnp.float32)).astype(jnp.bfloat16)
    return (normed, jnp.sqrt(ms), rows, key_new, value_new)


def spread(item, axis):
    return lax.all_to_all(item, axis, split_axis=0, concat_axis=0, tiled=True)


def choose_own(row, wanted, dest_flat, like):
    hits = dest_flat[None, :] == wanted[:, None]
    return jnp.sum(jnp.where(hits, row[None, :], 0.0), axis=1).astype(like)


def per_device(
    hidden_in,
    k_cache,
    v_cache,
    lengths,
    routes,
    w_query,
    b_query,
    w_key,
    b_key,
    w_value,
    b_value,
    w_out,
    gain_in,
    gain_out,
    w_head,
):
    n_rep = lax.axis_size("rep")
    n_tp = lax.axis_size("tp")
    rep_pos = lax.axis_index("rep")
    tp_pos = lax.axis_index("tp")
    part = tp_pos % 2
    slots = hidden_in.shape[0]
    cap = max(2, 2 * slots // n_rep)
    serve = n_rep * cap
    dest_flat, bucket_grid = destinations(routes, n_rep, slots, cap, serve)
    own_bucket = lax.dynamic_slice_in_dim(bucket_grid, rep_pos, 1, 0)[0]
    keys_home = k_cache[:, 0]
    values_home = v_cache[:, 0]
    weights_all = (w_query, b_query, w_key, b_key, w_value, b_value, w_out, gain_in, gain_out)
    send_k, send_v = fill_buckets((keys_home, values_home), own_bucket, serve, slots)
    got_k, got_v = spread(send_k, "rep"), spread(send_v, "rep")
    home_lens = lax.dynamic_slice_in_dim(lengths, rep_pos * slots, slots, 0)
    normed, norm_own, rows, key_new, value_new = layer(
        hidden_in, keys_home, values_home, home_lens, *weights_all, tp_pos, n_tp
    )
    (send_new,) = fill_buckets(
        (jnp.concatenate([key_new, value_new], axis=1),), own_bucket, serve, slots
    )
    got_new = spread(send_new, "rep")
    head_size = key_new.shape[1]
    targets = rep_pos * serve + jnp.arange(serve, dtype=jnp.int32)
    home, valid = find_home(dest_flat, targets)
    lens = jnp.where(valid, lengths[home], 0)
    keys_served = write_newest(got_k, got_new[:, :head_size], lens, valid, part)
    values_served = write_newest(got_v, got_new[:, head_size:], lens, valid, part)
    logits = lax.dot_general(
        w_head,
        lax.all_gather(normed, ("rep", "tp"), axis=0, tiled=True),
        (((1,), (1,)), ((), ())),
        preferred_element_type=jnp.float32,
    )
    norm_all = lax.dynamic_update_slice_in_dim(
        jnp.zeros((n_rep * slots,), jnp.float32),
        norm_own,
        (rep_pos * n_tp + tp_pos) * rows,
        0,
    )
    both = lax.pmax(jnp.stack([jnp.max(logits, axis=0), norm_all]), ("rep", "tp"))
    share = serve // n_tp
    wanted = (rep_pos * n_tp + tp_pos) * share + jnp.arange(share, dtype=jnp.int32)
    final_norm = choose_own(both[1], wanted, dest_flat, jnp.float32)
    top_logit = choose_own(both[0], wanted, dest_flat, jnp.float32)
    return (final_norm, top_logit, keys_served[:, None], values_served[:, None])


MESH = pl.DeviceIdType.MESH


def fused(
    n_rep,
    n_tp,
    pick,
    hid,
    cosf,
    sinf,
    lens,
    onehot,
    vecs,
    k_hbm,
    v_hbm,
    wq_hbm,
    wk_hbm,
    wv_hbm,
    wo_hbm,
    wh_hbm,
    out_k,
    out_v,
    out_new,
    out_max,
    kz,
    vz,
    kb,
    vb,
    wq,
    wk,
    wv,
    wo,
    wh,
    xf_s,
    pair,
    mixed_s,
    mixed_r,
    nb,
    rs_s,
    rs_b,
    rs_r,
    ag,
    xs,
    top_s,
    top_r,
    top2_s,
    top2_r,
    load_sem,
    keep_sem,
    cs,
    cr,
    ns,
    nr,
    ps,
    pr,
    rss,
    rsr,
    ags,
    agr,
    ts,
    tr,
):
    f32, bf16 = jnp.float32, jnp.bfloat16
    eps = 1e-06
    rep = lax.axis_index("rep")
    tp = lax.axis_index("tp")
    z, x = rep // 2, rep % 2
    y, c = tp // 2, tp % 2
    slots, d = hid.shape
    half_len, hd = kz.shape[1:]
    cap = kb.shape[0] // n_rep
    rows = slots // n_tp
    half_d = d // 2
    mate = tp + 1 - 2 * c
    me = rep * n_tp + tp

    def remote(src, dst, send, recv, rep_to, tp_to):
        return pltpu.make_async_remote_copy(
            src_ref=src,
            dst_ref=dst,
            send_sem=send,
            recv_sem=recv,
            device_id=(rep_to, tp_to),
            device_id_type=MESH,
        )

    loads = [
        pltpu.make_async_copy(src, dst, load_sem.at[i])
        for i, (src, dst) in enumerate(
            [
                (k_hbm, kz.at[pl.ds(0, slots)]),
                (v_hbm, vz.at[pl.ds(0, slots)]),
                (wq_hbm, wq),
                (wk_hbm, wk),
                (wv_hbm, wv),
                (wo_hbm, wo),
                (wh_hbm, wh),
            ]
        )
    ]
    for item in loads:
        item.start()
    kz[slots] = jnp.zeros((half_len, hd), bf16)
    vz[slots] = jnp.zeros((half_len, hd), bf16)

    barrier = pltpu.get_barrier_semaphore()
    for s in range(1, n_rep):
        pl.semaphore_signal(
            barrier, inc=1, device_id=((rep + s) % n_rep, tp), device_id_type=MESH
        )
    for s in range(1, n_tp):
        pl.semaphore_signal(
            barrier, inc=1, device_id=(rep, (tp + s) % n_tp), device_id_type=MESH
        )
    pl.semaphore_wait(barrier, n_rep - 1 + n_tp - 1)

    sends = []
    own = pl.ds(rep * cap, cap)
    caches = ((kz, kb, out_k), (vz, vb, out_v))

    def dispatch(which, shifts):
        src, buf, out = caches[which]
        for s in shifts:
            to = (rep + s) % n_rep

            def fill(j, carry, to=to):
                buf[to * cap + j] = src[pick[to * cap + j]]
                return carry

            lax.fori_loop(0, cap, fill, 0)
            there = pl.ds(to * cap, cap)
            if s:
                copy = remote(
                    buf.at[there], out.at[own], cs.at[which, s], cr.at[which, s], to, tp
                )
            else:
                copy = pltpu.make_async_copy(buf.at[own], out.at[own], keep_sem.at[which])
            copy.start()
            sends.append(copy)

    loads[0].wait()
    dispatch(0, (4, 3, 5, 2, 6, 1, 7, 0))

    xf = hid[...].astype(f32)
    xf_s[...] = xf
    scale_in = lax.rsqrt(jnp.mean(xf * xf, axis=1, keepdims=True) + eps)
    normed_in = (xf * scale_in * vecs[:, :d]).astype(bf16)
    cos, sin = cosf[...], sinf[...]

    def turn(vals):
        return vals * cos + pltpu.roll(vals, hd // 2, 1) * sin

    loads[2].wait()
    query = jnp.dot(normed_in, wq[...], preferred_element_type=f32) + vecs[:, 2 * d : 2 * d + 2 * hd]
    loads[3].wait()
    across = (((1,), (1,)), ((), ()))
    key_part = lax.dot_general(normed_in, wk[...], across, preferred_element_type=f32)
    loads[4].wait()
    value_part = lax.dot_general(normed_in, wv[...], across, preferred_element_type=f32)
    new_part = jnp.concatenate([key_part, value_part], axis=1) + vecs[:, 2 * d + 2 * hd :]
    pair[c] = jnp.concatenate(
        [
            turn(query[:, :hd]),
            turn(query[:, hd:]),
            new_part,
        ],
        axis=0,
    ).astype(bf16)
    swap = remote(pair.at[c], pair.at[c], ps.at[0], pr.at[0], rep, mate)
    swap.start()

    swap.wait_send()
    remote(pair.at[1 - c], pair.at[1 - c], ps.at[0], pr.at[0], rep, mate).wait_recv()
    first = pair[0].astype(f32)
    second = pair[1].astype(f32)
    queries = jnp.concatenate([first[: 2 * slots], second[: 2 * slots]], axis=0)
    key_raw = jnp.concatenate(
        [first[2 * slots :, : hd // 2], second[2 * slots :, : hd // 2]], axis=1
    )
    value_new = jnp.concatenate(
        [first[2 * slots :, hd // 2 :], second[2 * slots :, hd // 2 :]], axis=1
    )
    key_new = turn(key_raw).astype(bf16).astype(f32)
    new_k = jnp.dot(onehot[...], key_new.astype(bf16), preferred_element_type=f32)
    new_v = jnp.dot(onehot[...], value_new.astype(bf16), preferred_element_type=f32)
    for t in range(n_rep):
        cut = slice(t * cap, (t + 1) * cap)
        nb[t] = jnp.concatenate([new_k[cut], new_v[cut]], axis=0).astype(bf16)
    new_sends = []
    for s in range(1, n_rep):
        to = (rep + s) % n_rep
        copy = remote(nb.at[to], out_new.at[rep], ns.at[s], nr.at[s], to, tp)
        copy.start()
        new_sends.append(copy)
    out_new[rep] = nb[rep]

    count = 4 * slots
    scale = 1.0 / hd**0.5
    keys = kz[0:slots].reshape(slots * half_len, hd)
    loads[1].wait()
    values = vz[0:slots].reshape(slots * half_len, hd)
    scores = (
        lax.dot_general(
            queries.astype(bf16), keys, (((1,), (1,)), ((), ())), preferred_element_type=f32
        )
        * scale
    )
    row = lax.broadcasted_iota(jnp.int32, scores.shape, 0)
    col = lax.broadcasted_iota(jnp.int32, scores.shape, 1)
    live = (col // half_len == row % slots) & (col % half_len + c * half_len < lens[...])
    scores = jnp.where(live, scores, -1e30)
    own_score = (
        jnp.sum(queries * jnp.concatenate([key_new] * 4, axis=0), axis=1, keepdims=True) * scale
    )
    even = jnp.broadcast_to(c, (count, 1)) == 0
    own_score = jnp.where(even, own_score, -1e30)
    peak = jnp.maximum(jnp.max(scores, axis=1, keepdims=True), own_score)
    weights = jnp.where(live, jnp.exp(scores - peak), 0.0)
    own_weight = jnp.where(even, jnp.exp(own_score - peak), 0.0)
    total = jnp.sum(weights, axis=1, keepdims=True) + own_weight
    high = weights.astype(bf16)
    low = (weights - high.astype(f32)).astype(bf16)
    mixed = jnp.dot(high, values, preferred_element_type=f32) + jnp.dot(
        low, values, preferred_element_type=f32
    )
    mixed = mixed + own_weight * jnp.concatenate([value_new] * 4, axis=0)
    lane = lax.broadcasted_iota(jnp.int32, (count, hd), 1)
    stats = jnp.where(lane < hd // 2, peak, total)
    both = jnp.concatenate([mixed, stats], axis=1)
    mixed_s[0] = both[: 2 * slots]
    mixed_s[1] = both[2 * slots :]
    swap = remote(mixed_s.at[1 - c], mixed_r, ps.at[1], pr.at[1], rep, mate)
    swap.start()
    swap.wait()
    keep = mixed_s[c]
    got = mixed_r[...]
    peak_keep, total_keep = keep[:, hd : hd + 1], keep[:, 2 * hd - 1 : 2 * hd]
    peak_got, total_got = got[:, hd : hd + 1], got[:, 2 * hd - 1 : 2 * hd]
    upper = jnp.maximum(peak_keep, peak_got)
    mine = jnp.exp(peak_keep - upper)
    theirs = jnp.exp(peak_got - upper)
    merged = (keep[:, :hd] * mine + got[:, :hd] * theirs) / (
        total_keep * mine + total_got * theirs
    )
    attn = jnp.concatenate([merged[:slots], merged[slots:]], axis=1).astype(bf16)

    loads[5].wait()
    projected = jnp.dot(attn, wo[...], preferred_element_type=f32)
    for t in range(n_tp):
        cut = projected[t * rows : (t + 1) * rows]
        rs_s[t] = jnp.concatenate([cut[:, :half_d], cut[:, half_d:]], axis=0)
    for t in range(n_tp):
        rs_b[t] = rs_s[t].astype(bf16)
    rs_sends = []
    for s in range(1, n_tp):
        to = (tp + s) % n_tp
        copy = remote(rs_b.at[to], rs_r.at[s], rss.at[s], rsr.at[s], rep, to)
        copy.start()
        rs_sends.append(copy)
    summed = rs_s[tp]
    for s, copy in enumerate(rs_sends):
        copy.wait()
        summed = summed + rs_r[s + 1].astype(f32)
    own_x = xf_s[pl.ds(tp * rows, rows)]
    state = (
        (own_x + jnp.concatenate([summed[:rows], summed[rows:]], axis=1)).astype(bf16).astype(f32)
    )
    ms = jnp.mean(state * state, axis=1, keepdims=True)
    normed = state * lax.rsqrt(ms + eps) * vecs[:, d : 2 * d]
    ag[me] = jnp.concatenate([normed[:, :half_d], normed[:, half_d:]], axis=0).astype(bf16)

    x1, y1 = 1 - x, 1 - y
    rep_x = rep + 1 - 2 * x
    tp_y = tp + 2 - 4 * y
    rep_first, tp_first = c * rep + (1 - c) * rep_x, (1 - c) * tp + c * tp_y
    rep_second, tp_second = (1 - c) * rep + c * rep_x, c * tp + (1 - c) * tp_y
    x_first, x_second = c * x + (1 - c) * x1, (1 - c) * x + c * x1
    n_z = n_rep // 2
    base_b, base_c, base_d = n_z, 2 * n_z, 4 * n_z
    ag_sends = []

    def push(block, at, rep_to, tp_to):
        copy = remote(ag.at[block], ag.at[block], ags.at[at], agr.at[at], rep_to, tp_to)
        copy.start()
        ag_sends.append(copy)

    def arrived(block, at):
        remote(ag.at[block], ag.at[block], ags.at[at], agr.at[at], rep, mate).wait_recv()

    for s in range(1, n_z):
        push(me, s, ((z + s) % n_z) * 2 + x, tp)
    dispatch(1, range(2, n_rep, 2))
    plane = [(z + n_z - s) % n_z for s in range(n_z)]
    for s in range(n_z):
        block = (plane[s] * 2 + x) * n_tp + tp
        if s:
            arrived(block, s)
        push(block, base_b + s, rep_first, tp_first)
        push(block, base_c + s, rep_second, tp_second)
        push(block, base_d + s, rep, mate)
    for s in range(n_z):
        block = (plane[s] * 2 + x_first) * n_tp + tp_first
        arrived(block, base_b + s)
        push(block, base_c + n_z + s, rep_second, tp_second)
        push(block, base_d + n_z + s, rep, mate)
    dispatch(1, [3, 5, 1, 7, 0])
    for s in range(n_z):
        block = (plane[s] * 2 + x_second) * n_tp + tp_second
        arrived(block, base_c + s)
        push(block, base_d + 2 * n_z + s, rep, mate)
    for s in range(n_z):
        block = (plane[s] * 2 + x1) * n_tp + tp_y
        arrived(block, base_c + n_z + s)
        push(block, base_d + 3 * n_z + s, rep, mate)
    other_y = mate + 2 - 4 * y
    x_first_m, x_second_m = x_second, x_first
    tp_first_m = c * mate + (1 - c) * other_y
    tp_second_m = (1 - c) * mate + c * other_y
    for s in range(n_z):
        arrived((plane[s] * 2 + x) * n_tp + mate, base_d + s)
        arrived((plane[s] * 2 + x_first_m) * n_tp + tp_first_m, base_d + n_z + s)
        arrived((plane[s] * 2 + x_second_m) * n_tp + tp_second_m, base_d + 2 * n_z + s)
        arrived((plane[s] * 2 + x1) * n_tp + other_y, base_d + 3 * n_z + s)
    for copy in ag_sends:
        copy.wait_send()

    reqs = n_rep * slots
    width = 256
    for i in range(half_d // width):
        part = ag[:, :, i * width : (i + 1) * width].astype(f32)
        for h in range(2):
            xs[:, h * half_d + i * width : h * half_d + (i + 1) * width] = (
                part[:, h * rows : (h + 1) * rows].reshape(reqs, width).astype(bf16)
            )
    loads[6].wait()
    vocab = wh.shape[0]
    cuts = list(range(0, vocab, 208)) + [vocab]
    best = None
    for low_at, high_at in zip(cuts[:-1], cuts[1:]):
        logits = lax.dot_general(
            wh[low_at:high_at], xs[...], (((1,), (1,)), ((), ())), preferred_element_type=f32
        )
        one = jnp.max(logits, axis=0, keepdims=True)
        best = one if best is None else jnp.maximum(best, one)
    at_row = lax.broadcasted_iota(jnp.int32, (rows, reqs), 0)
    at_lane = lax.broadcasted_iota(jnp.int32, (rows, reqs), 1)
    rms = jnp.max(
        jnp.where(at_lane == at_row + me * rows, jnp.sqrt(ms), 0.0), axis=0, keepdims=True
    )
    top = jnp.where(at_row == 0, best, rms)
    top_s[...] = top
    hops = []
    for s in range(1, n_rep):
        copy = remote(top_s, top_r.at[s], ts.at[s], tr.at[s], (rep + s) % n_rep, tp)
        copy.start()
        hops.append(copy)
    for s, copy in enumerate(hops):
        copy.wait()
        top = jnp.maximum(top, top_r[s + 1])
    top2_s[...] = top
    hops = []
    for s in range(1, n_tp):
        at = n_rep + s
        copy = remote(top2_s, top2_r.at[s], ts.at[at], tr.at[at], rep, (tp + s) % n_tp)
        copy.start()
        hops.append(copy)
    for s, copy in enumerate(hops):
        copy.wait()
        top = jnp.maximum(top, top2_r[s + 1])
    out_max[...] = top

    for copy in new_sends:
        copy.wait()
    for copy in sends:
        copy.wait()


def fast_device(
    hidden_in,
    k_cache,
    v_cache,
    lengths,
    routes,
    w_query,
    b_query,
    w_key,
    b_key,
    w_value,
    b_value,
    w_out,
    gain_in,
    gain_out,
    w_head,
):
    n_rep = lax.axis_size("rep")
    n_tp = lax.axis_size("tp")
    rep_pos = lax.axis_index("rep")
    tp_pos = lax.axis_index("tp")
    part = tp_pos % 2
    slots, width = hidden_in.shape
    half_len, hd = k_cache.shape[2:]
    cap = max(2, 2 * slots // n_rep)
    serve = n_rep * cap
    rows = slots // n_tp
    reqs = n_rep * slots
    flat = routes[:, 0].reshape(n_rep, slots)
    order = jnp.arange(slots, dtype=jnp.int32)
    before = (flat[:, :, None] == flat[:, None, :]) & (order[None, None, :] < order[None, :, None])
    rank = jnp.sum(before.astype(jnp.int32), axis=2)
    source = jnp.arange(n_rep, dtype=jnp.int32)[:, None]
    dest_flat = (flat * serve + source * cap + rank).reshape(-1)
    own_bucket = lax.dynamic_slice_in_dim(flat * cap + rank, rep_pos, 1, 0)[0]
    hits = own_bucket[None, :] == jnp.arange(serve, dtype=jnp.int32)[:, None]
    pick = slots + jnp.sum(jnp.where(hits, order[None, :] - slots, 0), axis=1)
    onehot = hits.astype(jnp.bfloat16)
    home_lens = lax.dynamic_slice_in_dim(lengths, rep_pos * slots, slots, 0)
    freq = 1000000.0 ** (-(jnp.arange(hd // 2, dtype=jnp.float32) * 2.0 / hd))
    angle = home_lens.astype(jnp.float32)[:, None] * freq
    cos, sin = jnp.cos(angle), jnp.sin(angle)
    cosf = jnp.concatenate([cos, cos], axis=1)
    sinf = jnp.concatenate([-sin, sin], axis=1)
    bf16, f32 = jnp.bfloat16, jnp.float32
    vmem = pl.BlockSpec(memory_space=pltpu.VMEM)
    anywhere = pl.BlockSpec(memory_space=pl.ANY)
    dma = pltpu.SemaphoreType.DMA
    block = (2 * rows, width // 2)
    got_k, got_v, got_new, best = pl.pallas_call(
        functools.partial(fused, n_rep, n_tp),
        out_shape=[
            jax.ShapeDtypeStruct((serve, half_len, hd), bf16),
            jax.ShapeDtypeStruct((serve, half_len, hd), bf16),
            jax.ShapeDtypeStruct((n_rep, 2 * cap, hd), bf16),
            jax.ShapeDtypeStruct((8, reqs), f32),
        ],
        in_specs=[pl.BlockSpec(memory_space=pltpu.SMEM)] + [vmem] * 6 + [anywhere] * 7,
        out_specs=[anywhere, anywhere, vmem, vmem],
        scratch_shapes=[
            pltpu.VMEM((slots + 1, half_len, hd), bf16),
            pltpu.VMEM((slots + 1, half_len, hd), bf16),
            pltpu.VMEM((serve, half_len, hd), bf16),
            pltpu.VMEM((serve, half_len, hd), bf16),
            pltpu.VMEM(w_query.shape, bf16),
            pltpu.VMEM(w_key.shape[::-1], bf16),
            pltpu.VMEM(w_value.shape[::-1], bf16),
            pltpu.VMEM(w_out.shape, bf16),
            pltpu.VMEM(w_head.shape, bf16),
            pltpu.VMEM((slots, width), f32),
            pltpu.VMEM((2, 3 * slots, hd), bf16),
            pltpu.VMEM((2, 2 * slots, 2 * hd), f32),
            pltpu.VMEM((2 * slots, 2 * hd), f32),
            pltpu.VMEM((n_rep, 2 * cap, hd), bf16),
            pltpu.VMEM((n_tp,) + block, f32),
            pltpu.VMEM((n_tp,) + block, bf16),
            pltpu.VMEM((n_tp,) + block, bf16),
            pltpu.VMEM((n_rep * n_tp,) + block, bf16),
            pltpu.VMEM((reqs, width), bf16),
            pltpu.VMEM((8, reqs), f32),
            pltpu.VMEM((n_rep, 8, reqs), f32),
            pltpu.VMEM((8, reqs), f32),
            pltpu.VMEM((n_tp, 8, reqs), f32),
            dma((7,)),
            dma((2,)),
            dma((2, n_rep)),
            dma((2, n_rep)),
            dma((n_rep,)),
            dma((n_rep,)),
            dma((2,)),
            dma((2,)),
            dma((n_tp,)),
            dma((n_tp,)),
            dma((4 * n_rep,)),
            dma((4 * n_rep,)),
            dma((n_rep + n_tp,)),
            dma((n_rep + n_tp,)),
        ],
        compiler_params=pltpu.CompilerParams(
            collective_id=0, has_side_effects=True, vmem_limit_bytes=60 * 1024 * 1024
        ),
    )(
        pick,
        hidden_in,
        cosf,
        sinf,
        jnp.tile(home_lens, 4)[:, None],
        onehot,
        jnp.concatenate([gain_in, gain_out, b_query, b_key, b_value]).astype(f32)[None],
        k_cache[:, 0],
        v_cache[:, 0],
        w_query,
        w_key.T,
        w_value.T,
        w_out,
        w_head,
    )
    new = got_new.reshape(n_rep, 2, cap, hd)
    new_k = new[:, 0].reshape(serve, hd)
    new_v = new[:, 1].reshape(serve, hd)
    targets = rep_pos * serve + jnp.arange(serve, dtype=jnp.int32)
    equal = dest_flat[None, :] == targets[:, None]
    lens = jnp.sum(jnp.where(equal, lengths[None, :] + 1, 0), axis=1) - 1
    valid = lens >= 0
    keys_served = write_newest(got_k, new_k, lens, valid, part)
    values_served = write_newest(got_v, new_v, lens, valid, part)
    share = serve // n_tp
    wanted = (rep_pos * n_tp + tp_pos) * share + jnp.arange(share, dtype=jnp.int32)
    final_norm = choose_own(best[1], wanted, dest_flat, f32)
    top_logit = choose_own(best[0], wanted, dest_flat, f32)
    return (final_norm, top_logit, keys_served[:, None], values_served[:, None])


def solution(mesh):
    in_specs = (
        P("rep", None),
        P("rep", "tp", None, None),
        P("rep", "tp", None, None),
        P(),
        P(),
        P(None, "tp"),
        P("tp"),
        P(None, "tp"),
        P("tp"),
        P(None, "tp"),
        P("tp"),
        P("tp", None),
        P(),
        P(),
        P(("rep", "tp"), None),
    )
    out_specs = (
        P(("rep", "tp")),
        P(("rep", "tp")),
        P("rep", "tp", None, None),
        P("rep", "tp", None, None),
    )
    small = mesh.shape["rep"] == 8 and mesh.shape["tp"] == 4
    return jax.shard_map(
        fast_device if small else per_device, mesh=mesh, in_specs=in_specs, out_specs=out_specs, check_vma=False
    )
```

```python
import functools
import math

import jax
import jax.numpy as jnp
from jax import lax
from jax.experimental import pallas as pl
from jax.experimental.pallas import tpu as pltpu
from jax.sharding import PartitionSpec as P


def swapped(shard, axis, distance):
    return lax.ppermute(shard, axis, [(i, i ^ 1 << distance) for i in range(lax.axis_size(axis))])


def rotate(vals, positions):
    half = vals.shape[-1] // 2
    freq = 1000000.0 ** (-(jnp.arange(half, dtype=jnp.float32) * 2.0 / vals.shape[-1]))
    angle = positions[..., None] * freq
    first = vals[..., :half]
    second = vals[..., half:]
    return jnp.concatenate(
        [
            first * jnp.cos(angle) - second * jnp.sin(angle),
            second * jnp.cos(angle) + first * jnp.sin(angle),
        ],
        axis=-1,
    )


def destinations(routes, n_rep, slots, cap, serve):
    flat = routes[:, 0].reshape(n_rep, slots)
    onehot = (flat[:, :, None] == jnp.arange(n_rep, dtype=jnp.int32)[None, None, :]).astype(
        jnp.int32
    )
    rank = jnp.sum((jnp.cumsum(onehot, axis=1) - onehot) * onehot, axis=2)
    source = jnp.arange(n_rep, dtype=jnp.int32)[:, None]
    return ((flat * serve + source * cap + rank).reshape(-1), flat * cap + rank)


def find_home(dest_flat, targets):
    equal = dest_flat[None, :] == targets[:, None]
    home = jnp.sum(
        jnp.where(equal, jnp.arange(dest_flat.shape[0], dtype=jnp.int32)[None, :], 0), axis=1
    )
    return (home, jnp.any(equal, axis=1))


def fill_buckets(arrays, own_bucket, serve, slots):
    hits = own_bucket[None, :] == jnp.arange(serve, dtype=jnp.int32)[:, None]
    pick = jnp.sum(jnp.where(hits, jnp.arange(slots, dtype=jnp.int32)[None, :], 0), axis=1)
    filled = jnp.any(hits, axis=1)
    return tuple(
        [
            jnp.where(
                filled.reshape((-1,) + (1,) * (item.ndim - 1)),
                item[pick],
                jnp.zeros((), item.dtype),
            )
            for item in arrays
        ]
    )


def write_newest(stored, newest, lens, live_rows, part):
    half_len = stored.shape[1]
    where_pos = part * half_len + jnp.arange(half_len, dtype=jnp.int32)
    written = (where_pos[None, :] == lens[:, None]) & live_rows[:, None]
    return jnp.where(written[:, :, None], newest[:, None, :], stored)


def layer(
    xs,
    keys,
    values,
    lens,
    w_query,
    b_query,
    w_key,
    b_key,
    w_value,
    b_value,
    w_out,
    gain_in,
    gain_out,
    tp_pos,
    n_tp,
):
    eps = 1e-06
    count = xs.shape[0]
    head_size = keys.shape[-1]
    half_len = keys.shape[1]
    part = tp_pos % 2
    even = part == 0
    xf = xs.astype(jnp.float32)
    normed_in = (
        xf * lax.rsqrt(jnp.mean(xf * xf, axis=1, keepdims=True) + eps) * gain_in.astype(jnp.float32)
    ).astype(jnp.bfloat16)
    positions = lens.astype(jnp.float32)[:, None]
    query = (
        jnp.dot(normed_in, w_query, preferred_element_type=jnp.float32)
        + b_query.astype(jnp.float32)
    ).reshape(count, -1, head_size)
    query = rotate(query, positions).astype(jnp.bfloat16)
    key_part = (
        jnp.dot(normed_in, w_key, preferred_element_type=jnp.float32) + b_key.astype(jnp.float32)
    ).astype(jnp.bfloat16)
    value_part = (
        jnp.dot(normed_in, w_value, preferred_element_type=jnp.float32)
        + b_value.astype(jnp.float32)
    ).astype(jnp.bfloat16)
    other_query, other_key, other_value = swapped((query, key_part, value_part), "tp", 0)
    queries = jnp.where(
        even,
        jnp.concatenate([query, other_query], axis=1),
        jnp.concatenate([other_query, query], axis=1),
    )
    key_raw = jnp.where(
        even,
        jnp.concatenate([key_part, other_key], axis=1),
        jnp.concatenate([other_key, key_part], axis=1),
    )
    value_new = jnp.where(
        even,
        jnp.concatenate([value_part, other_value], axis=1),
        jnp.concatenate([other_value, value_part], axis=1),
    )
    key_new = rotate(key_raw.astype(jnp.float32)[:, None, :], positions)[:, 0].astype(jnp.bfloat16)
    scale = 1.0 / head_size**0.5
    scores = jnp.einsum("sgd,spd->sgp", queries, keys, preferred_element_type=jnp.float32) * scale
    place = part * half_len + jnp.arange(half_len, dtype=jnp.int32)
    live = (place[None, :] < lens[:, None])[:, None, :]
    scores = jnp.where(live, scores, -1e30)
    own_score = (
        jnp.einsum("sgd,sd->sg", queries, key_new, preferred_element_type=jnp.float32) * scale
    )
    own_score = jnp.where(even, own_score, -1e30)
    peak = jnp.maximum(jnp.max(scores, axis=2), own_score)
    weights = jnp.where(live, jnp.exp(scores - peak[..., None]), 0.0)
    own_weight = jnp.where(even, jnp.exp(own_score - peak), 0.0)
    total = jnp.sum(weights, axis=2) + own_weight
    mixed = jnp.einsum(
        "sgp,spd->sgd", weights, values.astype(jnp.float32), precision=lax.Precision.HIGHEST
    )
    mixed = mixed + own_weight[..., None] * value_new.astype(jnp.float32)[:, None, :]
    mixed_keep = jnp.where(even, mixed[:, :2], mixed[:, 2:])
    mixed_give = jnp.where(even, mixed[:, 2:], mixed[:, :2])
    peak_keep = jnp.where(even, peak[:, :2], peak[:, 2:])
    peak_give = jnp.where(even, peak[:, 2:], peak[:, :2])
    total_keep = jnp.where(even, total[:, :2], total[:, 2:])
    total_give = jnp.where(even, total[:, 2:], total[:, :2])
    got_mixed, got_peak, got_total = swapped((mixed_give, peak_give, total_give), "tp", 0)
    upper = jnp.maximum(peak_keep, got_peak)
    mine = jnp.exp(peak_keep - upper)
    theirs = jnp.exp(got_peak - upper)
    merged = (mixed_keep * mine[..., None] + got_mixed * theirs[..., None]) / (
        total_keep * mine + got_total * theirs
    )[..., None]
    attn = merged.reshape(count, -1).astype(jnp.bfloat16)
    rows = count // n_tp
    projected = lax.psum_scatter(
        jnp.dot(attn, w_out, preferred_element_type=jnp.float32),
        "tp",
        scatter_dimension=0,
        tiled=True,
    )
    own_x = lax.dynamic_slice_in_dim(xf, tp_pos * rows, rows, 0)
    state = (own_x + projected).astype(jnp.bfloat16)
    sf = state.astype(jnp.float32)
    ms = jnp.mean(sf * sf, axis=1)
    normed = (sf * lax.rsqrt(ms + eps)[:, None] * gain_out.astype(jnp.float32)).astype(jnp.bfloat16)
    return (normed, jnp.sqrt(ms), rows, key_new, value_new)


def spread(item, axis):
    return lax.all_to_all(item, axis, split_axis=0, concat_axis=0, tiled=True)


def choose_own(row, wanted, dest_flat, like):
    hits = dest_flat[None, :] == wanted[:, None]
    return jnp.sum(jnp.where(hits, row[None, :], 0.0), axis=1).astype(like)


def per_device(
    hidden_in,
    k_cache,
    v_cache,
    lengths,
    routes,
    w_query,
    b_query,
    w_key,
    b_key,
    w_value,
    b_value,
    w_out,
    gain_in,
    gain_out,
    w_head,
):
    n_rep = lax.axis_size("rep")
    n_tp = lax.axis_size("tp")
    rep_pos = lax.axis_index("rep")
    tp_pos = lax.axis_index("tp")
    part = tp_pos % 2
    slots = hidden_in.shape[0]
    cap = max(2, 2 * slots // n_rep)
    serve = n_rep * cap
    dest_flat, bucket_grid = destinations(routes, n_rep, slots, cap, serve)
    own_bucket = lax.dynamic_slice_in_dim(bucket_grid, rep_pos, 1, 0)[0]
    keys_home = k_cache[:, 0]
    values_home = v_cache[:, 0]
    weights_all = (w_query, b_query, w_key, b_key, w_value, b_value, w_out, gain_in, gain_out)
    send_k, send_v = fill_buckets((keys_home, values_home), own_bucket, serve, slots)
    got_k, got_v = spread(send_k, "rep"), spread(send_v, "rep")
    home_lens = lax.dynamic_slice_in_dim(lengths, rep_pos * slots, slots, 0)
    normed, norm_own, rows, key_new, value_new = layer(
        hidden_in, keys_home, values_home, home_lens, *weights_all, tp_pos, n_tp
    )
    (send_new,) = fill_buckets(
        (jnp.concatenate([key_new, value_new], axis=1),), own_bucket, serve, slots
    )
    got_new = spread(send_new, "rep")
    head_size = key_new.shape[1]
    targets = rep_pos * serve + jnp.arange(serve, dtype=jnp.int32)
    home, valid = find_home(dest_flat, targets)
    lens = jnp.where(valid, lengths[home], 0)
    keys_served = write_newest(got_k, got_new[:, :head_size], lens, valid, part)
    values_served = write_newest(got_v, got_new[:, head_size:], lens, valid, part)
    logits = lax.dot_general(
        w_head,
        lax.all_gather(normed, ("rep", "tp"), axis=0, tiled=True),
        (((1,), (1,)), ((), ())),
        preferred_element_type=jnp.float32,
    )
    norm_all = lax.dynamic_update_slice_in_dim(
        jnp.zeros((n_rep * slots,), jnp.float32),
        norm_own,
        (rep_pos * n_tp + tp_pos) * rows,
        0,
    )
    both = lax.pmax(jnp.stack([jnp.max(logits, axis=0), norm_all]), ("rep", "tp"))
    share = serve // n_tp
    wanted = (rep_pos * n_tp + tp_pos) * share + jnp.arange(share, dtype=jnp.int32)
    final_norm = choose_own(both[1], wanted, dest_flat, jnp.float32)
    top_logit = choose_own(both[0], wanted, dest_flat, jnp.float32)
    return (final_norm, top_logit, keys_served[:, None], values_served[:, None])


MESH = pl.DeviceIdType.MESH


def fused(
    n_rep,
    n_tp,
    pick,
    lengths,
    hid,
    gin,
    gout,
    bq,
    bk,
    bv,
    k_hbm,
    v_hbm,
    wq_hbm,
    wk_hbm,
    wv_hbm,
    wo_hbm,
    wh_hbm,
    out_k,
    out_v,
    out_new,
    out_max,
    kz,
    vz,
    kb,
    vb,
    wq,
    wk,
    wv,
    wo,
    wh,
    xf_s,
    pair,
    new_s,
    mixed_s,
    mixed_r,
    nb,
    rs_s,
    rs_b,
    rs_r,
    ag,
    xs,
    top_s,
    top_r,
    top2_s,
    top2_r,
    load_sem,
    keep_sem,
    cs,
    cr,
    ns,
    nr,
    ps,
    pr,
    rss,
    rsr,
    ags,
    agr,
    ts,
    tr,
):
    f32, bf16 = jnp.float32, jnp.bfloat16
    eps = 1e-06
    rep = lax.axis_index("rep")
    tp = lax.axis_index("tp")
    z, x = rep // 2, rep % 2
    y, c = tp // 2, tp % 2
    slots, d = hid.shape
    half_len, hd = kz.shape[1:]
    cap = kb.shape[0] // n_rep
    rows = slots // n_tp
    half_d = d // 2
    mate = tp + 1 - 2 * c
    me = rep * n_tp + tp

    def vec(ref):
        return ref[...].astype(f32)[None, :]

    def remote(src, dst, send, recv, rep_to, tp_to):
        return pltpu.make_async_remote_copy(
            src_ref=src,
            dst_ref=dst,
            send_sem=send,
            recv_sem=recv,
            device_id=(rep_to, tp_to),
            device_id_type=MESH,
        )

    loads = [
        pltpu.make_async_copy(src, dst, load_sem.at[i])
        for i, (src, dst) in enumerate(
            [
                (k_hbm, kz.at[pl.ds(0, slots)]),
                (v_hbm, vz.at[pl.ds(0, slots)]),
                (wq_hbm, wq),
                (wk_hbm, wk),
                (wv_hbm, wv),
                (wo_hbm, wo),
                (wh_hbm, wh),
            ]
        )
    ]
    for item in loads:
        item.start()
    kz[slots] = jnp.zeros((half_len, hd), bf16)
    vz[slots] = jnp.zeros((half_len, hd), bf16)

    barrier = pltpu.get_barrier_semaphore()
    for s in range(1, n_rep):
        pl.semaphore_signal(
            barrier, inc=1, device_id=((rep + s) % n_rep, tp), device_id_type=MESH
        )
    for s in range(1, n_tp):
        pl.semaphore_signal(
            barrier, inc=1, device_id=(rep, (tp + s) % n_tp), device_id_type=MESH
        )
    pl.semaphore_wait(barrier, n_rep - 1 + n_tp - 1)

    sends = []
    own = pl.ds(rep * cap, cap)
    caches = ((kz, kb, out_k), (vz, vb, out_v))

    def dispatch(which, shifts):
        src, buf, out = caches[which]
        for s in shifts:
            to = (rep + s) % n_rep

            def fill(j, carry, to=to):
                buf[to * cap + j] = src[pick[to * cap + j]]
                return carry

            lax.fori_loop(0, cap, fill, 0)
            there = pl.ds(to * cap, cap)
            if s:
                copy = remote(
                    buf.at[there], out.at[own], cs.at[which, s], cr.at[which, s], to, tp
                )
            else:
                copy = pltpu.make_async_copy(buf.at[own], out.at[own], keep_sem.at[which])
            copy.start()
            sends.append(copy)

    loads[0].wait()
    dispatch(0, (4, 3, 5, 2, 6, 1, 7, 0))

    xf = hid[...].astype(f32)
    xf_s[...] = xf
    scale_in = lax.rsqrt(jnp.mean(xf * xf, axis=1, keepdims=True) + eps)
    normed_in = (xf * scale_in * vec(gin)).astype(bf16)
    place = lax.broadcasted_iota(jnp.int32, (slots, hd), 0)
    lens = jnp.zeros((slots, hd), jnp.int32)
    for s in range(slots):
        lens = jnp.where(place == s, lengths[rep * slots + s], lens)
    entry = lax.broadcasted_iota(jnp.int32, (slots, hd), 1)
    power = (entry % (hd // 2)).astype(f32) * (-2.0 / hd * math.log(1000000.0))
    angle = lens.astype(f32) * jnp.exp(power)
    cos, sin = jnp.cos(angle), jnp.sin(angle)
    sin = jnp.where(entry < hd // 2, -sin, sin)

    def turn(vals):
        return vals * cos + pltpu.roll(vals, hd // 2, 1) * sin

    loads[2].wait()
    query = jnp.dot(normed_in, wq[...], preferred_element_type=f32) + vec(bq)
    loads[3].wait()
    across = (((1,), (1,)), ((), ()))
    key_part = lax.dot_general(normed_in, wk[...], across, preferred_element_type=f32)
    loads[4].wait()
    value_part = lax.dot_general(normed_in, wv[...], across, preferred_element_type=f32)
    new_part = jnp.concatenate([key_part + vec(bk), value_part + vec(bv)], axis=1)
    pair[c] = jnp.concatenate(
        [
            turn(query[:, :hd]),
            turn(query[:, hd:]),
            new_part,
        ],
        axis=0,
    ).astype(bf16)
    swap = remote(pair.at[c], pair.at[c], ps.at[0], pr.at[0], rep, mate)
    swap.start()

    swap.wait_send()
    remote(pair.at[1 - c], pair.at[1 - c], ps.at[0], pr.at[0], rep, mate).wait_recv()
    first = pair[0].astype(f32)
    second = pair[1].astype(f32)
    queries = jnp.concatenate([first[: 2 * slots], second[: 2 * slots]], axis=0)
    key_raw = jnp.concatenate(
        [first[2 * slots :, : hd // 2], second[2 * slots :, : hd // 2]], axis=1
    )
    value_new = jnp.concatenate(
        [first[2 * slots :, hd // 2 :], second[2 * slots :, hd // 2 :]], axis=1
    )
    key_new = turn(key_raw).astype(bf16).astype(f32)
    new_s[0:slots] = jnp.concatenate([key_new, value_new], axis=1)
    new_s[slots : slots + 8] = jnp.zeros((8, 2 * hd), f32)

    def fill_new(j, carry):
        nb[pl.ds(j, 1)] = new_s[pl.ds(pick[j], 1)]
        return carry

    lax.fori_loop(0, n_rep * cap, fill_new, 0, unroll=8)
    new_sends = []
    for s in range(1, n_rep):
        to = (rep + s) % n_rep
        copy = remote(
            nb.at[pl.ds(to * cap, cap)], out_new.at[own], ns.at[s], nr.at[s], to, tp
        )
        copy.start()
        new_sends.append(copy)
    out_new[own] = nb[own]

    count = 4 * slots
    scale = 1.0 / hd**0.5
    keys = kz[0:slots].reshape(slots * half_len, hd)
    loads[1].wait()
    values = vz[0:slots].reshape(slots * half_len, hd)
    scores = (
        lax.dot_general(
            queries.astype(bf16), keys, (((1,), (1,)), ((), ())), preferred_element_type=f32
        )
        * scale
    )
    row = lax.broadcasted_iota(jnp.int32, scores.shape, 0)
    col = lax.broadcasted_iota(jnp.int32, scores.shape, 1)
    live = (col // half_len == row % slots) & (col % half_len + c * half_len < jnp.concatenate([lens[:, :1]] * 4, axis=0))
    scores = jnp.where(live, scores, -1e30)
    own_score = (
        jnp.sum(queries * jnp.concatenate([key_new] * 4, axis=0), axis=1, keepdims=True) * scale
    )
    even = jnp.broadcast_to(c, (count, 1)) == 0
    own_score = jnp.where(even, own_score, -1e30)
    peak = jnp.maximum(jnp.max(scores, axis=1, keepdims=True), own_score)
    weights = jnp.where(live, jnp.exp(scores - peak), 0.0)
    own_weight = jnp.where(even, jnp.exp(own_score - peak), 0.0)
    total = jnp.sum(weights, axis=1, keepdims=True) + own_weight
    high = weights.astype(bf16)
    low = (weights - high.astype(f32)).astype(bf16)
    mixed = jnp.dot(high, values, preferred_element_type=f32) + jnp.dot(
        low, values, preferred_element_type=f32
    )
    mixed = mixed + own_weight * jnp.concatenate([value_new] * 4, axis=0)
    lane = lax.broadcasted_iota(jnp.int32, (count, hd), 1)
    stats = jnp.where(lane < hd // 2, peak, total)
    both = jnp.concatenate([mixed, stats], axis=1)
    mixed_s[0] = both[: 2 * slots]
    mixed_s[1] = both[2 * slots :]
    swap = remote(mixed_s.at[1 - c], mixed_r, ps.at[1], pr.at[1], rep, mate)
    swap.start()
    swap.wait()
    keep = mixed_s[c]
    got = mixed_r[...]
    peak_keep, total_keep = keep[:, hd : hd + 1], keep[:, 2 * hd - 1 : 2 * hd]
    peak_got, total_got = got[:, hd : hd + 1], got[:, 2 * hd - 1 : 2 * hd]
    upper = jnp.maximum(peak_keep, peak_got)
    mine = jnp.exp(peak_keep - upper)
    theirs = jnp.exp(peak_got - upper)
    merged = (keep[:, :hd] * mine + got[:, :hd] * theirs) / (
        total_keep * mine + total_got * theirs
    )
    attn = jnp.concatenate([merged[:slots], merged[slots:]], axis=1).astype(bf16)

    loads[5].wait()
    projected = jnp.dot(attn, wo[...], preferred_element_type=f32)
    for t in range(n_tp):
        cut = projected[t * rows : (t + 1) * rows]
        rs_s[t] = jnp.concatenate([cut[:, :half_d], cut[:, half_d:]], axis=0)
    for t in range(n_tp):
        rs_b[t] = rs_s[t].astype(bf16)
    rs_sends = []
    for s in range(1, n_tp):
        to = (tp + s) % n_tp
        copy = remote(rs_b.at[to], rs_r.at[s], rss.at[s], rsr.at[s], rep, to)
        copy.start()
        rs_sends.append(copy)
    summed = rs_s[tp]
    for s, copy in enumerate(rs_sends):
        copy.wait()
        summed = summed + rs_r[s + 1].astype(f32)
    own_x = xf_s[pl.ds(tp * rows, rows)]
    state = (
        (own_x + jnp.concatenate([summed[:rows], summed[rows:]], axis=1)).astype(bf16).astype(f32)
    )
    ms = jnp.mean(state * state, axis=1, keepdims=True)
    normed = state * lax.rsqrt(ms + eps) * vec(gout)
    ag[me] = jnp.concatenate([normed[:, :half_d], normed[:, half_d:]], axis=0).astype(bf16)

    x1, y1 = 1 - x, 1 - y
    rep_x = rep + 1 - 2 * x
    tp_y = tp + 2 - 4 * y
    rep_first, tp_first = c * rep + (1 - c) * rep_x, (1 - c) * tp + c * tp_y
    rep_second, tp_second = (1 - c) * rep + c * rep_x, c * tp + (1 - c) * tp_y
    x_first, x_second = c * x + (1 - c) * x1, (1 - c) * x + c * x1
    n_z = n_rep // 2
    base_b, base_c, base_d = n_z, 2 * n_z, 4 * n_z
    ag_sends = []

    def push(block, at, rep_to, tp_to):
        copy = remote(ag.at[block], ag.at[block], ags.at[at], agr.at[at], rep_to, tp_to)
        copy.start()
        ag_sends.append(copy)

    def arrived(block, at):
        remote(ag.at[block], ag.at[block], ags.at[at], agr.at[at], rep, mate).wait_recv()

    for s in range(1, n_z):
        push(me, s, ((z + s) % n_z) * 2 + x, tp)
    plane = [(z + n_z - s) % n_z for s in range(n_z)]
    for s in range(n_z):
        block = (plane[s] * 2 + x) * n_tp + tp
        if s:
            arrived(block, s)
        push(block, base_b + s, rep_first, tp_first)
        push(block, base_c + s, rep_second, tp_second)
        push(block, base_d + s, rep, mate)
    dispatch(1, (4, 2, 6))
    for s in range(n_z):
        block = (plane[s] * 2 + x_first) * n_tp + tp_first
        arrived(block, base_b + s)
        push(block, base_c + n_z + s, rep_second, tp_second)
        push(block, base_d + n_z + s, rep, mate)
    for s in range(n_z):
        block = (plane[s] * 2 + x_second) * n_tp + tp_second
        arrived(block, base_c + s)
        push(block, base_d + 2 * n_z + s, rep, mate)
    for s in range(n_z):
        block = (plane[s] * 2 + x1) * n_tp + tp_y
        arrived(block, base_c + n_z + s)
        push(block, base_d + 3 * n_z + s, rep, mate)
    dispatch(1, (3, 5, 1, 7, 0))
    other_y = mate + 2 - 4 * y
    x_first_m, x_second_m = x_second, x_first
    tp_first_m = c * mate + (1 - c) * other_y
    tp_second_m = (1 - c) * mate + c * other_y
    for s in range(n_z):
        arrived((plane[s] * 2 + x) * n_tp + mate, base_d + s)
        arrived((plane[s] * 2 + x_first_m) * n_tp + tp_first_m, base_d + n_z + s)
        arrived((plane[s] * 2 + x_second_m) * n_tp + tp_second_m, base_d + 2 * n_z + s)
        arrived((plane[s] * 2 + x1) * n_tp + other_y, base_d + 3 * n_z + s)
    for copy in ag_sends:
        copy.wait_send()

    reqs = n_rep * slots
    width = 256
    for i in range(half_d // width):
        part = ag[:, :, i * width : (i + 1) * width].astype(f32)
        for h in range(2):
            xs[:, h * half_d + i * width : h * half_d + (i + 1) * width] = (
                part[:, h * rows : (h + 1) * rows].reshape(reqs, width).astype(bf16)
            )
    loads[6].wait()
    vocab = wh.shape[0]
    cuts = list(range(0, vocab, 208)) + [vocab]
    best = None
    for low_at, high_at in zip(cuts[:-1], cuts[1:]):
        logits = lax.dot_general(
            wh[low_at:high_at], xs[...], (((1,), (1,)), ((), ())), preferred_element_type=f32
        )
        one = jnp.max(logits, axis=0, keepdims=True)
        best = one if best is None else jnp.maximum(best, one)
    at_row = lax.broadcasted_iota(jnp.int32, (rows, reqs), 0)
    at_lane = lax.broadcasted_iota(jnp.int32, (rows, reqs), 1)
    rms = jnp.max(
        jnp.where(at_lane == at_row + me * rows, jnp.sqrt(ms), 0.0), axis=0, keepdims=True
    )
    top = jnp.where(at_row == 0, best, rms)
    top_s[...] = top
    hops = []
    for s in range(1, n_rep):
        copy = remote(top_s, top_r.at[s], ts.at[s], tr.at[s], (rep + s) % n_rep, tp)
        copy.start()
        hops.append(copy)
    for s, copy in enumerate(hops):
        copy.wait()
        top = jnp.maximum(top, top_r[s + 1])
    top2_s[...] = top
    hops = []
    for s in range(1, n_tp):
        at = n_rep + s
        copy = remote(top2_s, top2_r.at[s], ts.at[at], tr.at[at], rep, (tp + s) % n_tp)
        copy.start()
        hops.append(copy)
    for s, copy in enumerate(hops):
        copy.wait()
        top = jnp.maximum(top, top2_r[s + 1])
    out_max[...] = top

    for copy in new_sends:
        copy.wait()
    for copy in sends:
        copy.wait()


def fast_device(
    hidden_in,
    k_cache,
    v_cache,
    lengths,
    routes,
    w_query,
    b_query,
    w_key,
    b_key,
    w_value,
    b_value,
    w_out,
    gain_in,
    gain_out,
    w_head,
):
    n_rep = lax.axis_size("rep")
    n_tp = lax.axis_size("tp")
    rep_pos = lax.axis_index("rep")
    tp_pos = lax.axis_index("tp")
    part = tp_pos % 2
    slots, width = hidden_in.shape
    half_len, hd = k_cache.shape[2:]
    cap = max(2, 2 * slots // n_rep)
    serve = n_rep * cap
    rows = slots // n_tp
    reqs = n_rep * slots
    flat = routes[:, 0].reshape(n_rep, slots)
    order = jnp.arange(slots, dtype=jnp.int32)
    before = (flat[:, :, None] == flat[:, None, :]) & (order[None, None, :] < order[None, :, None])
    rank = jnp.sum(before.astype(jnp.int32), axis=2)
    source = jnp.arange(n_rep, dtype=jnp.int32)[:, None]
    dest_flat = (flat * serve + source * cap + rank).reshape(-1)
    own_bucket = lax.dynamic_slice_in_dim(flat * cap + rank, rep_pos, 1, 0)[0]
    hits = own_bucket[None, :] == jnp.arange(serve, dtype=jnp.int32)[:, None]
    pick = slots + jnp.sum(jnp.where(hits, order[None, :] - slots, 0), axis=1)
    bf16, f32 = jnp.bfloat16, jnp.float32
    vmem = pl.BlockSpec(memory_space=pltpu.VMEM)
    anywhere = pl.BlockSpec(memory_space=pl.ANY)
    dma = pltpu.SemaphoreType.DMA
    block = (2 * rows, width // 2)
    got_k, got_v, got_new, best = pl.pallas_call(
        functools.partial(fused, n_rep, n_tp),
        out_shape=[
            jax.ShapeDtypeStruct((serve, half_len, hd), bf16),
            jax.ShapeDtypeStruct((serve, half_len, hd), bf16),
            jax.ShapeDtypeStruct((serve, 2 * hd), f32),
            jax.ShapeDtypeStruct((8, reqs), f32),
        ],
        in_specs=[pl.BlockSpec(memory_space=pltpu.SMEM)] * 2 + [vmem] * 6 + [anywhere] * 7,
        out_specs=[anywhere, anywhere, vmem, vmem],
        scratch_shapes=[
            pltpu.VMEM((slots + 1, half_len, hd), bf16),
            pltpu.VMEM((slots + 1, half_len, hd), bf16),
            pltpu.VMEM((serve, half_len, hd), bf16),
            pltpu.VMEM((serve, half_len, hd), bf16),
            pltpu.VMEM(w_query.shape, bf16),
            pltpu.VMEM(w_key.shape[::-1], bf16),
            pltpu.VMEM(w_value.shape[::-1], bf16),
            pltpu.VMEM(w_out.shape, bf16),
            pltpu.VMEM(w_head.shape, bf16),
            pltpu.VMEM((slots, width), f32),
            pltpu.VMEM((2, 3 * slots, hd), bf16),
            pltpu.VMEM((slots + 8, 2 * hd), f32),
            pltpu.VMEM((2, 2 * slots, 2 * hd), f32),
            pltpu.VMEM((2 * slots, 2 * hd), f32),
            pltpu.VMEM((serve, 2 * hd), f32),
            pltpu.VMEM((n_tp,) + block, f32),
            pltpu.VMEM((n_tp,) + block, bf16),
            pltpu.VMEM((n_tp,) + block, bf16),
            pltpu.VMEM((n_rep * n_tp,) + block, bf16),
            pltpu.VMEM((reqs, width), bf16),
            pltpu.VMEM((8, reqs), f32),
            pltpu.VMEM((n_rep, 8, reqs), f32),
            pltpu.VMEM((8, reqs), f32),
            pltpu.VMEM((n_tp, 8, reqs), f32),
            dma((7,)),
            dma((2,)),
            dma((2, n_rep)),
            dma((2, n_rep)),
            dma((n_rep,)),
            dma((n_rep,)),
            dma((2,)),
            dma((2,)),
            dma((n_tp,)),
            dma((n_tp,)),
            dma((4 * n_rep,)),
            dma((4 * n_rep,)),
            dma((n_rep + n_tp,)),
            dma((n_rep + n_tp,)),
        ],
        compiler_params=pltpu.CompilerParams(
            collective_id=0, has_side_effects=True, vmem_limit_bytes=60 * 1024 * 1024
        ),
    )(
        pick,
        lengths,
        hidden_in,
        gain_in,
        gain_out,
        b_query,
        b_key,
        b_value,
        k_cache[:, 0],
        v_cache[:, 0],
        w_query,
        w_key.T,
        w_value.T,
        w_out,
        w_head,
    )
    got_new = got_new.astype(bf16)
    new_k, new_v = got_new[:, :hd], got_new[:, hd:]
    targets = rep_pos * serve + jnp.arange(serve, dtype=jnp.int32)
    equal = dest_flat[None, :] == targets[:, None]
    lens = jnp.sum(jnp.where(equal, lengths[None, :] + 1, 0), axis=1) - 1
    valid = lens >= 0
    keys_served = write_newest(got_k, new_k, lens, valid, part)
    values_served = write_newest(got_v, new_v, lens, valid, part)
    share = serve // n_tp
    wanted = (rep_pos * n_tp + tp_pos) * share + jnp.arange(share, dtype=jnp.int32)
    final_norm = choose_own(best[1], wanted, dest_flat, f32)
    top_logit = choose_own(best[0], wanted, dest_flat, f32)
    return (final_norm, top_logit, keys_served[:, None], values_served[:, None])


def solution(mesh):
    in_specs = (
        P("rep", None),
        P("rep", "tp", None, None),
        P("rep", "tp", None, None),
        P(),
        P(),
        P(None, "tp"),
        P("tp"),
        P(None, "tp"),
        P("tp"),
        P(None, "tp"),
        P("tp"),
        P("tp", None),
        P(),
        P(),
        P(("rep", "tp"), None),
    )
    out_specs = (
        P(("rep", "tp")),
        P(("rep", "tp")),
        P("rep", "tp", None, None),
        P("rep", "tp", None, None),
    )
    small = mesh.shape["rep"] == 8 and mesh.shape["tp"] == 4
    return jax.shard_map(
        fast_device if small else per_device, mesh=mesh, in_specs=in_specs, out_specs=out_specs, check_vma=False
    )
```

```python
import functools
import math

import jax
import jax.numpy as jnp
from jax import lax
from jax.experimental import pallas as pl
from jax.experimental.pallas import tpu as pltpu
from jax.sharding import PartitionSpec as P


def swapped(shard, axis, distance):
    return lax.ppermute(shard, axis, [(i, i ^ 1 << distance) for i in range(lax.axis_size(axis))])


def rotate(vals, positions):
    half = vals.shape[-1] // 2
    freq = 1000000.0 ** (-(jnp.arange(half, dtype=jnp.float32) * 2.0 / vals.shape[-1]))
    angle = positions[..., None] * freq
    first = vals[..., :half]
    second = vals[..., half:]
    return jnp.concatenate(
        [
            first * jnp.cos(angle) - second * jnp.sin(angle),
            second * jnp.cos(angle) + first * jnp.sin(angle),
        ],
        axis=-1,
    )


def destinations(routes, n_rep, slots, cap, serve):
    flat = routes[:, 0].reshape(n_rep, slots)
    onehot = (flat[:, :, None] == jnp.arange(n_rep, dtype=jnp.int32)[None, None, :]).astype(
        jnp.int32
    )
    rank = jnp.sum((jnp.cumsum(onehot, axis=1) - onehot) * onehot, axis=2)
    source = jnp.arange(n_rep, dtype=jnp.int32)[:, None]
    return ((flat * serve + source * cap + rank).reshape(-1), flat * cap + rank)


def find_home(dest_flat, targets):
    equal = dest_flat[None, :] == targets[:, None]
    home = jnp.sum(
        jnp.where(equal, jnp.arange(dest_flat.shape[0], dtype=jnp.int32)[None, :], 0), axis=1
    )
    return (home, jnp.any(equal, axis=1))


def fill_buckets(arrays, own_bucket, serve, slots):
    hits = own_bucket[None, :] == jnp.arange(serve, dtype=jnp.int32)[:, None]
    pick = jnp.sum(jnp.where(hits, jnp.arange(slots, dtype=jnp.int32)[None, :], 0), axis=1)
    filled = jnp.any(hits, axis=1)
    return tuple(
        [
            jnp.where(
                filled.reshape((-1,) + (1,) * (item.ndim - 1)),
                item[pick],
                jnp.zeros((), item.dtype),
            )
            for item in arrays
        ]
    )


def write_newest(stored, newest, lens, live_rows, part):
    half_len = stored.shape[1]
    where_pos = part * half_len + jnp.arange(half_len, dtype=jnp.int32)
    written = (where_pos[None, :] == lens[:, None]) & live_rows[:, None]
    return jnp.where(written[:, :, None], newest[:, None, :], stored)


def layer(
    xs,
    keys,
    values,
    lens,
    w_query,
    b_query,
    w_key,
    b_key,
    w_value,
    b_value,
    w_out,
    gain_in,
    gain_out,
    tp_pos,
    n_tp,
):
    eps = 1e-06
    count = xs.shape[0]
    head_size = keys.shape[-1]
    half_len = keys.shape[1]
    part = tp_pos % 2
    even = part == 0
    xf = xs.astype(jnp.float32)
    normed_in = (
        xf * lax.rsqrt(jnp.mean(xf * xf, axis=1, keepdims=True) + eps) * gain_in.astype(jnp.float32)
    ).astype(jnp.bfloat16)
    positions = lens.astype(jnp.float32)[:, None]
    query = (
        jnp.dot(normed_in, w_query, preferred_element_type=jnp.float32)
        + b_query.astype(jnp.float32)
    ).reshape(count, -1, head_size)
    query = rotate(query, positions).astype(jnp.bfloat16)
    key_part = (
        jnp.dot(normed_in, w_key, preferred_element_type=jnp.float32) + b_key.astype(jnp.float32)
    ).astype(jnp.bfloat16)
    value_part = (
        jnp.dot(normed_in, w_value, preferred_element_type=jnp.float32)
        + b_value.astype(jnp.float32)
    ).astype(jnp.bfloat16)
    other_query, other_key, other_value = swapped((query, key_part, value_part), "tp", 0)
    queries = jnp.where(
        even,
        jnp.concatenate([query, other_query], axis=1),
        jnp.concatenate([other_query, query], axis=1),
    )
    key_raw = jnp.where(
        even,
        jnp.concatenate([key_part, other_key], axis=1),
        jnp.concatenate([other_key, key_part], axis=1),
    )
    value_new = jnp.where(
        even,
        jnp.concatenate([value_part, other_value], axis=1),
        jnp.concatenate([other_value, value_part], axis=1),
    )
    key_new = rotate(key_raw.astype(jnp.float32)[:, None, :], positions)[:, 0].astype(jnp.bfloat16)
    scale = 1.0 / head_size**0.5
    scores = jnp.einsum("sgd,spd->sgp", queries, keys, preferred_element_type=jnp.float32) * scale
    place = part * half_len + jnp.arange(half_len, dtype=jnp.int32)
    live = (place[None, :] < lens[:, None])[:, None, :]
    scores = jnp.where(live, scores, -1e30)
    own_score = (
        jnp.einsum("sgd,sd->sg", queries, key_new, preferred_element_type=jnp.float32) * scale
    )
    own_score = jnp.where(even, own_score, -1e30)
    peak = jnp.maximum(jnp.max(scores, axis=2), own_score)
    weights = jnp.where(live, jnp.exp(scores - peak[..., None]), 0.0)
    own_weight = jnp.where(even, jnp.exp(own_score - peak), 0.0)
    total = jnp.sum(weights, axis=2) + own_weight
    mixed = jnp.einsum(
        "sgp,spd->sgd", weights, values.astype(jnp.float32), precision=lax.Precision.HIGHEST
    )
    mixed = mixed + own_weight[..., None] * value_new.astype(jnp.float32)[:, None, :]
    mixed_keep = jnp.where(even, mixed[:, :2], mixed[:, 2:])
    mixed_give = jnp.where(even, mixed[:, 2:], mixed[:, :2])
    peak_keep = jnp.where(even, peak[:, :2], peak[:, 2:])
    peak_give = jnp.where(even, peak[:, 2:], peak[:, :2])
    total_keep = jnp.where(even, total[:, :2], total[:, 2:])
    total_give = jnp.where(even, total[:, 2:], total[:, :2])
    got_mixed, got_peak, got_total = swapped((mixed_give, peak_give, total_give), "tp", 0)
    upper = jnp.maximum(peak_keep, got_peak)
    mine = jnp.exp(peak_keep - upper)
    theirs = jnp.exp(got_peak - upper)
    merged = (mixed_keep * mine[..., None] + got_mixed * theirs[..., None]) / (
        total_keep * mine + got_total * theirs
    )[..., None]
    attn = merged.reshape(count, -1).astype(jnp.bfloat16)
    rows = count // n_tp
    projected = lax.psum_scatter(
        jnp.dot(attn, w_out, preferred_element_type=jnp.float32),
        "tp",
        scatter_dimension=0,
        tiled=True,
    )
    own_x = lax.dynamic_slice_in_dim(xf, tp_pos * rows, rows, 0)
    state = (own_x + projected).astype(jnp.bfloat16)
    sf = state.astype(jnp.float32)
    ms = jnp.mean(sf * sf, axis=1)
    normed = (sf * lax.rsqrt(ms + eps)[:, None] * gain_out.astype(jnp.float32)).astype(jnp.bfloat16)
    return (normed, jnp.sqrt(ms), rows, key_new, value_new)


def spread(item, axis):
    return lax.all_to_all(item, axis, split_axis=0, concat_axis=0, tiled=True)


def choose_own(row, wanted, dest_flat, like):
    hits = dest_flat[None, :] == wanted[:, None]
    return jnp.sum(jnp.where(hits, row[None, :], 0.0), axis=1).astype(like)


def per_device(
    hidden_in,
    k_cache,
    v_cache,
    lengths,
    routes,
    w_query,
    b_query,
    w_key,
    b_key,
    w_value,
    b_value,
    w_out,
    gain_in,
    gain_out,
    w_head,
):
    n_rep = lax.axis_size("rep")
    n_tp = lax.axis_size("tp")
    rep_pos = lax.axis_index("rep")
    tp_pos = lax.axis_index("tp")
    part = tp_pos % 2
    slots = hidden_in.shape[0]
    cap = max(2, 2 * slots // n_rep)
    serve = n_rep * cap
    dest_flat, bucket_grid = destinations(routes, n_rep, slots, cap, serve)
    own_bucket = lax.dynamic_slice_in_dim(bucket_grid, rep_pos, 1, 0)[0]
    keys_home = k_cache[:, 0]
    values_home = v_cache[:, 0]
    weights_all = (w_query, b_query, w_key, b_key, w_value, b_value, w_out, gain_in, gain_out)
    send_k, send_v = fill_buckets((keys_home, values_home), own_bucket, serve, slots)
    got_k, got_v = spread(send_k, "rep"), spread(send_v, "rep")
    home_lens = lax.dynamic_slice_in_dim(lengths, rep_pos * slots, slots, 0)
    normed, norm_own, rows, key_new, value_new = layer(
        hidden_in, keys_home, values_home, home_lens, *weights_all, tp_pos, n_tp
    )
    (send_new,) = fill_buckets(
        (jnp.concatenate([key_new, value_new], axis=1),), own_bucket, serve, slots
    )
    got_new = spread(send_new, "rep")
    head_size = key_new.shape[1]
    targets = rep_pos * serve + jnp.arange(serve, dtype=jnp.int32)
    home, valid = find_home(dest_flat, targets)
    lens = jnp.where(valid, lengths[home], 0)
    keys_served = write_newest(got_k, got_new[:, :head_size], lens, valid, part)
    values_served = write_newest(got_v, got_new[:, head_size:], lens, valid, part)
    logits = lax.dot_general(
        w_head,
        lax.all_gather(normed, ("rep", "tp"), axis=0, tiled=True),
        (((1,), (1,)), ((), ())),
        preferred_element_type=jnp.float32,
    )
    norm_all = lax.dynamic_update_slice_in_dim(
        jnp.zeros((n_rep * slots,), jnp.float32),
        norm_own,
        (rep_pos * n_tp + tp_pos) * rows,
        0,
    )
    both = lax.pmax(jnp.stack([jnp.max(logits, axis=0), norm_all]), ("rep", "tp"))
    share = serve // n_tp
    wanted = (rep_pos * n_tp + tp_pos) * share + jnp.arange(share, dtype=jnp.int32)
    final_norm = choose_own(both[1], wanted, dest_flat, jnp.float32)
    top_logit = choose_own(both[0], wanted, dest_flat, jnp.float32)
    return (final_norm, top_logit, keys_served[:, None], values_served[:, None])


MESH = pl.DeviceIdType.MESH


def fused(
    n_rep,
    n_tp,
    pick,
    lengths,
    hid,
    gin,
    gout,
    bq,
    bk,
    bv,
    k_hbm,
    v_hbm,
    wq_hbm,
    wk_hbm,
    wv_hbm,
    wo_hbm,
    wh_hbm,
    out_k,
    out_v,
    out_nk,
    out_nv,
    out_max,
    kz,
    vz,
    kb,
    vb,
    wq,
    wk,
    wv,
    wo,
    wh,
    xf_s,
    pair,
    new_s,
    new_r,
    mixed_s,
    mixed_r,
    nb,
    rs_s,
    rs_b,
    rs_r,
    ag,
    xs,
    top_s,
    top_r,
    top2_s,
    top2_r,
    load_sem,
    keep_sem,
    cs,
    cr,
    ns,
    nr,
    ps,
    pr,
    rss,
    rsr,
    ags,
    agr,
    ts,
    tr,
):
    f32, bf16 = jnp.float32, jnp.bfloat16
    eps = 1e-06
    rep = lax.axis_index("rep")
    tp = lax.axis_index("tp")
    z, x = rep // 2, rep % 2
    y, c = tp // 2, tp % 2
    slots, d = hid.shape
    half_len, hd = kz.shape[1:]
    cap = kb.shape[0] // n_rep
    rows = slots // n_tp
    half_d = d // 2
    mate = tp + 1 - 2 * c
    me = rep * n_tp + tp

    def vec(ref):
        return ref[...].astype(f32)[None, :]

    def remote(src, dst, send, recv, rep_to, tp_to):
        return pltpu.make_async_remote_copy(
            src_ref=src,
            dst_ref=dst,
            send_sem=send,
            recv_sem=recv,
            device_id=(rep_to, tp_to),
            device_id_type=MESH,
        )

    loads = [
        pltpu.make_async_copy(src, dst, load_sem.at[i])
        for i, (src, dst) in enumerate(
            [
                (k_hbm, kz.at[pl.ds(0, slots)]),
                (v_hbm, vz.at[pl.ds(0, slots)]),
                (wq_hbm, wq),
                (wk_hbm, wk),
                (wv_hbm, wv),
                (wo_hbm, wo),
                (wh_hbm, wh),
            ]
        )
    ]
    for item in loads:
        item.start()
    kz[slots] = jnp.zeros((half_len, hd), bf16)
    vz[slots] = jnp.zeros((half_len, hd), bf16)

    barrier = pltpu.get_barrier_semaphore()
    for s in range(1, n_rep):
        pl.semaphore_signal(
            barrier, inc=1, device_id=((rep + s) % n_rep, tp), device_id_type=MESH
        )
    for s in range(1, n_tp):
        pl.semaphore_signal(
            barrier, inc=1, device_id=(rep, (tp + s) % n_tp), device_id_type=MESH
        )
    pl.semaphore_wait(barrier, n_rep - 1 + n_tp - 1)

    sends = []
    own = pl.ds(rep * cap, cap)
    caches = ((kz, kb, out_k), (vz, vb, out_v))

    def dispatch(which, shifts):
        src, buf, out = caches[which]
        for s in shifts:
            to = (rep + s) % n_rep

            def fill(j, carry, to=to):
                buf[to * cap + j] = src[pick[to * cap + j]]
                return carry

            lax.fori_loop(0, cap, fill, 0)
            there = pl.ds(to * cap, cap)
            if s:
                copy = remote(
                    buf.at[there], out.at[own], cs.at[which, s], cr.at[which, s], to, tp
                )
            else:
                copy = pltpu.make_async_copy(buf.at[own], out.at[own], keep_sem.at[which])
            copy.start()
            sends.append(copy)

    loads[0].wait()
    dispatch(0, (4, 3, 5, 2, 6, 1, 7, 0))

    xf = hid[...].astype(f32)
    xf_s[...] = xf
    scale_in = lax.rsqrt(jnp.mean(xf * xf, axis=1, keepdims=True) + eps)
    normed_in = (xf * scale_in * vec(gin)).astype(bf16)
    place = lax.broadcasted_iota(jnp.int32, (slots, hd), 0)
    lens = jnp.zeros((slots, hd), jnp.int32)
    for s in range(slots):
        lens = jnp.where(place == s, lengths[rep * slots + s], lens)
    entry = lax.broadcasted_iota(jnp.int32, (slots, hd), 1)
    power = (entry % (hd // 2)).astype(f32) * (-2.0 / hd * math.log(1000000.0))
    angle = lens.astype(f32) * jnp.exp(power)
    cos, sin = jnp.cos(angle), jnp.sin(angle)
    sin = jnp.where(entry < hd // 2, -sin, sin)

    def turn(vals):
        return vals * cos + pltpu.roll(vals, hd // 2, 1) * sin

    loads[2].wait()
    query = jnp.dot(normed_in, wq[...], preferred_element_type=f32) + vec(bq)
    loads[3].wait()
    across = (((1,), (1,)), ((), ()))
    key_part = lax.dot_general(normed_in, wk[...], across, preferred_element_type=f32)
    loads[4].wait()
    value_part = lax.dot_general(normed_in, wv[...], across, preferred_element_type=f32)
    new_part = jnp.concatenate([key_part + vec(bk), value_part + vec(bv)], axis=1)
    pair[c] = jnp.concatenate(
        [
            turn(query[:, :hd]),
            turn(query[:, hd:]),
            new_part,
        ],
        axis=0,
    ).astype(bf16)
    swap = remote(pair.at[c], pair.at[c], ps.at[0], pr.at[0], rep, mate)
    swap.start()

    swap.wait_send()
    remote(pair.at[1 - c], pair.at[1 - c], ps.at[0], pr.at[0], rep, mate).wait_recv()
    first = pair[0].astype(f32)
    second = pair[1].astype(f32)
    queries = jnp.concatenate([first[: 2 * slots], second[: 2 * slots]], axis=0)
    key_raw = jnp.concatenate(
        [first[2 * slots :, : hd // 2], second[2 * slots :, : hd // 2]], axis=1
    )
    value_new = jnp.concatenate(
        [first[2 * slots :, hd // 2 :], second[2 * slots :, hd // 2 :]], axis=1
    )
    key_new = turn(key_raw).astype(bf16).astype(f32)
    new_s[0:slots] = jnp.concatenate([key_new, value_new], axis=1)
    new_s[slots : slots + 8] = jnp.zeros((8, 2 * hd), f32)

    def fill_new(j, carry):
        nb[pl.ds(j, 1)] = new_s[pl.ds(pick[j], 1)]
        return carry

    lax.fori_loop(0, n_rep * cap, fill_new, 0, unroll=8)
    new_sends = []
    for s in range(1, n_rep):
        to = (rep + s) % n_rep
        copy = remote(
            nb.at[pl.ds(to * cap, cap)], new_r.at[own], ns.at[s], nr.at[s], to, tp
        )
        copy.start()
        new_sends.append(copy)
    new_r[own] = nb[own]

    count = 4 * slots
    scale = 1.0 / hd**0.5
    keys = kz[0:slots].reshape(slots * half_len, hd)
    loads[1].wait()
    values = vz[0:slots].reshape(slots * half_len, hd)
    scores = (
        lax.dot_general(
            queries.astype(bf16), keys, (((1,), (1,)), ((), ())), preferred_element_type=f32
        )
        * scale
    )
    row = lax.broadcasted_iota(jnp.int32, scores.shape, 0)
    col = lax.broadcasted_iota(jnp.int32, scores.shape, 1)
    live = (col // half_len == row % slots) & (col % half_len + c * half_len < jnp.concatenate([lens[:, :1]] * 4, axis=0))
    scores = jnp.where(live, scores, -1e30)
    own_score = (
        jnp.sum(queries * jnp.concatenate([key_new] * 4, axis=0), axis=1, keepdims=True) * scale
    )
    even = jnp.broadcast_to(c, (count, 1)) == 0
    own_score = jnp.where(even, own_score, -1e30)
    peak = jnp.maximum(jnp.max(scores, axis=1, keepdims=True), own_score)
    weights = jnp.where(live, jnp.exp(scores - peak), 0.0)
    own_weight = jnp.where(even, jnp.exp(own_score - peak), 0.0)
    total = jnp.sum(weights, axis=1, keepdims=True) + own_weight
    high = weights.astype(bf16)
    low = (weights - high.astype(f32)).astype(bf16)
    mixed = jnp.dot(high, values, preferred_element_type=f32) + jnp.dot(
        low, values, preferred_element_type=f32
    )
    mixed = mixed + own_weight * jnp.concatenate([value_new] * 4, axis=0)
    lane = lax.broadcasted_iota(jnp.int32, (count, hd), 1)
    stats = jnp.where(lane < hd // 2, peak, total)
    both = jnp.concatenate([mixed, stats], axis=1)
    mixed_s[0] = both[: 2 * slots]
    mixed_s[1] = both[2 * slots :]
    swap = remote(mixed_s.at[1 - c], mixed_r, ps.at[1], pr.at[1], rep, mate)
    swap.start()
    swap.wait()
    keep = mixed_s[c]
    got = mixed_r[...]
    peak_keep, total_keep = keep[:, hd : hd + 1], keep[:, 2 * hd - 1 : 2 * hd]
    peak_got, total_got = got[:, hd : hd + 1], got[:, 2 * hd - 1 : 2 * hd]
    upper = jnp.maximum(peak_keep, peak_got)
    mine = jnp.exp(peak_keep - upper)
    theirs = jnp.exp(peak_got - upper)
    merged = (keep[:, :hd] * mine + got[:, :hd] * theirs) / (
        total_keep * mine + total_got * theirs
    )
    attn = jnp.concatenate([merged[:slots], merged[slots:]], axis=1).astype(bf16)

    loads[5].wait()
    projected = jnp.dot(attn, wo[...], preferred_element_type=f32)
    for t in range(n_tp):
        cut = projected[t * rows : (t + 1) * rows]
        rs_s[t] = jnp.concatenate([cut[:, :half_d], cut[:, half_d:]], axis=0)
    for t in range(n_tp):
        rs_b[t] = rs_s[t].astype(bf16)
    rs_sends = []
    for s in range(1, n_tp):
        to = (tp + s) % n_tp
        copy = remote(rs_b.at[to], rs_r.at[s], rss.at[s], rsr.at[s], rep, to)
        copy.start()
        rs_sends.append(copy)
    summed = rs_s[tp]
    for s, copy in enumerate(rs_sends):
        copy.wait()
        summed = summed + rs_r[s + 1].astype(f32)
    own_x = xf_s[pl.ds(tp * rows, rows)]
    state = (
        (own_x + jnp.concatenate([summed[:rows], summed[rows:]], axis=1)).astype(bf16).astype(f32)
    )
    ms = jnp.mean(state * state, axis=1, keepdims=True)
    normed = state * lax.rsqrt(ms + eps) * vec(gout)
    ag[me] = jnp.concatenate([normed[:, :half_d], normed[:, half_d:]], axis=0).astype(bf16)

    x1, y1 = 1 - x, 1 - y
    rep_x = rep + 1 - 2 * x
    tp_y = tp + 2 - 4 * y
    rep_first, tp_first = c * rep + (1 - c) * rep_x, (1 - c) * tp + c * tp_y
    rep_second, tp_second = (1 - c) * rep + c * rep_x, c * tp + (1 - c) * tp_y
    x_first, x_second = c * x + (1 - c) * x1, (1 - c) * x + c * x1
    n_z = n_rep // 2
    base_b, base_c, base_d = n_z, 2 * n_z, 4 * n_z
    ag_sends = []

    def push(block, at, rep_to, tp_to):
        copy = remote(ag.at[block], ag.at[block], ags.at[at], agr.at[at], rep_to, tp_to)
        copy.start()
        ag_sends.append(copy)

    def arrived(block, at):
        remote(ag.at[block], ag.at[block], ags.at[at], agr.at[at], rep, mate).wait_recv()

    for s in range(1, n_z):
        push(me, s, ((z + s) % n_z) * 2 + x, tp)
    plane = [(z + n_z - s) % n_z for s in range(n_z)]
    for s in range(n_z):
        block = (plane[s] * 2 + x) * n_tp + tp
        if s:
            arrived(block, s)
        push(block, base_b + s, rep_first, tp_first)
        push(block, base_c + s, rep_second, tp_second)
        push(block, base_d + s, rep, mate)
    dispatch(1, (4, 2, 6))
    for s in range(n_z):
        block = (plane[s] * 2 + x_first) * n_tp + tp_first
        arrived(block, base_b + s)
        push(block, base_c + n_z + s, rep_second, tp_second)
        push(block, base_d + n_z + s, rep, mate)
    for s in range(n_z):
        block = (plane[s] * 2 + x_second) * n_tp + tp_second
        arrived(block, base_c + s)
        push(block, base_d + 2 * n_z + s, rep, mate)
    for s in range(n_z):
        block = (plane[s] * 2 + x1) * n_tp + tp_y
        arrived(block, base_c + n_z + s)
        push(block, base_d + 3 * n_z + s, rep, mate)
    dispatch(1, (3, 5, 1, 7, 0))
    other_y = mate + 2 - 4 * y
    x_first_m, x_second_m = x_second, x_first
    tp_first_m = c * mate + (1 - c) * other_y
    tp_second_m = (1 - c) * mate + c * other_y
    for s in range(n_z):
        arrived((plane[s] * 2 + x) * n_tp + mate, base_d + s)
        arrived((plane[s] * 2 + x_first_m) * n_tp + tp_first_m, base_d + n_z + s)
        arrived((plane[s] * 2 + x_second_m) * n_tp + tp_second_m, base_d + 2 * n_z + s)
        arrived((plane[s] * 2 + x1) * n_tp + other_y, base_d + 3 * n_z + s)
    for copy in ag_sends:
        copy.wait_send()

    reqs = n_rep * slots
    width = 256
    for i in range(half_d // width):
        part = ag[:, :, i * width : (i + 1) * width].astype(f32)
        for h in range(2):
            xs[:, h * half_d + i * width : h * half_d + (i + 1) * width] = (
                part[:, h * rows : (h + 1) * rows].reshape(reqs, width).astype(bf16)
            )
    loads[6].wait()
    vocab = wh.shape[0]
    cuts = list(range(0, vocab, 208)) + [vocab]
    best = None
    for low_at, high_at in zip(cuts[:-1], cuts[1:]):
        logits = lax.dot_general(
            wh[low_at:high_at], xs[...], (((1,), (1,)), ((), ())), preferred_element_type=f32
        )
        one = jnp.max(logits, axis=0, keepdims=True)
        best = one if best is None else jnp.maximum(best, one)
    at_row = lax.broadcasted_iota(jnp.int32, (rows, reqs), 0)
    at_lane = lax.broadcasted_iota(jnp.int32, (rows, reqs), 1)
    rms = jnp.max(
        jnp.where(at_lane == at_row + me * rows, jnp.sqrt(ms), 0.0), axis=0, keepdims=True
    )
    top = jnp.where(at_row == 0, best, rms)
    top_s[...] = top
    hops = []
    for s in range(1, n_rep):
        copy = remote(top_s, top_r.at[s], ts.at[s], tr.at[s], (rep + s) % n_rep, tp)
        copy.start()
        hops.append(copy)
    for s, copy in enumerate(hops):
        copy.wait()
        top = jnp.maximum(top, top_r[s + 1])
    top2_s[...] = top
    hops = []
    for s in range(1, n_tp):
        at = n_rep + s
        copy = remote(top2_s, top2_r.at[s], ts.at[at], tr.at[at], rep, (tp + s) % n_tp)
        copy.start()
        hops.append(copy)
    for s, copy in enumerate(hops):
        copy.wait()
        top = jnp.maximum(top, top2_r[s + 1])
    out_max[...] = top

    for copy in new_sends:
        copy.wait()
    out_nk[...] = new_r[:, :hd].astype(bf16)
    out_nv[...] = new_r[:, hd:].astype(bf16)
    for copy in sends:
        copy.wait()


def fast_device(
    hidden_in,
    k_cache,
    v_cache,
    lengths,
    routes,
    w_query,
    b_query,
    w_key,
    b_key,
    w_value,
    b_value,
    w_out,
    gain_in,
    gain_out,
    w_head,
):
    n_rep = lax.axis_size("rep")
    n_tp = lax.axis_size("tp")
    rep_pos = lax.axis_index("rep")
    tp_pos = lax.axis_index("tp")
    part = tp_pos % 2
    slots, width = hidden_in.shape
    half_len, hd = k_cache.shape[2:]
    cap = max(2, 2 * slots // n_rep)
    serve = n_rep * cap
    rows = slots // n_tp
    reqs = n_rep * slots
    flat = routes[:, 0].reshape(n_rep, slots)
    order = jnp.arange(slots, dtype=jnp.int32)
    before = (flat[:, :, None] == flat[:, None, :]) & (order[None, None, :] < order[None, :, None])
    rank = jnp.sum(before.astype(jnp.int32), axis=2)
    source = jnp.arange(n_rep, dtype=jnp.int32)[:, None]
    dest_flat = (flat * serve + source * cap + rank).reshape(-1)
    own_bucket = lax.dynamic_slice_in_dim(flat * cap + rank, rep_pos, 1, 0)[0]
    hits = own_bucket[None, :] == jnp.arange(serve, dtype=jnp.int32)[:, None]
    pick = slots + jnp.sum(jnp.where(hits, order[None, :] - slots, 0), axis=1)
    bf16, f32 = jnp.bfloat16, jnp.float32
    vmem = pl.BlockSpec(memory_space=pltpu.VMEM)
    anywhere = pl.BlockSpec(memory_space=pl.ANY)
    dma = pltpu.SemaphoreType.DMA
    block = (2 * rows, width // 2)
    got_k, got_v, new_k, new_v, best = pl.pallas_call(
        functools.partial(fused, n_rep, n_tp),
        out_shape=[
            jax.ShapeDtypeStruct((serve, half_len, hd), bf16),
            jax.ShapeDtypeStruct((serve, half_len, hd), bf16),
            jax.ShapeDtypeStruct((serve, hd), bf16),
            jax.ShapeDtypeStruct((serve, hd), bf16),
            jax.ShapeDtypeStruct((8, reqs), f32),
        ],
        in_specs=[pl.BlockSpec(memory_space=pltpu.SMEM)] * 2 + [vmem] * 6 + [anywhere] * 7,
        out_specs=[anywhere, anywhere, vmem, vmem, vmem],
        scratch_shapes=[
            pltpu.VMEM((slots + 1, half_len, hd), bf16),
            pltpu.VMEM((slots + 1, half_len, hd), bf16),
            pltpu.VMEM((serve, half_len, hd), bf16),
            pltpu.VMEM((serve, half_len, hd), bf16),
            pltpu.VMEM(w_query.shape, bf16),
            pltpu.VMEM(w_key.shape[::-1], bf16),
            pltpu.VMEM(w_value.shape[::-1], bf16),
            pltpu.VMEM(w_out.shape, bf16),
            pltpu.VMEM(w_head.shape, bf16),
            pltpu.VMEM((slots, width), f32),
            pltpu.VMEM((2, 3 * slots, hd), bf16),
            pltpu.VMEM((slots + 8, 2 * hd), f32),
            pltpu.VMEM((serve, 2 * hd), f32),
            pltpu.VMEM((2, 2 * slots, 2 * hd), f32),
            pltpu.VMEM((2 * slots, 2 * hd), f32),
            pltpu.VMEM((serve, 2 * hd), f32),
            pltpu.VMEM((n_tp,) + block, f32),
            pltpu.VMEM((n_tp,) + block, bf16),
            pltpu.VMEM((n_tp,) + block, bf16),
            pltpu.VMEM((n_rep * n_tp,) + block, bf16),
            pltpu.VMEM((reqs, width), bf16),
            pltpu.VMEM((8, reqs), f32),
            pltpu.VMEM((n_rep, 8, reqs), f32),
            pltpu.VMEM((8, reqs), f32),
            pltpu.VMEM((n_tp, 8, reqs), f32),
            dma((7,)),
            dma((2,)),
            dma((2, n_rep)),
            dma((2, n_rep)),
            dma((n_rep,)),
            dma((n_rep,)),
            dma((2,)),
            dma((2,)),
            dma((n_tp,)),
            dma((n_tp,)),
            dma((4 * n_rep,)),
            dma((4 * n_rep,)),
            dma((n_rep + n_tp,)),
            dma((n_rep + n_tp,)),
        ],
        compiler_params=pltpu.CompilerParams(
            collective_id=0, has_side_effects=True, vmem_limit_bytes=60 * 1024 * 1024
        ),
    )(
        pick,
        lengths,
        hidden_in,
        gain_in,
        gain_out,
        b_query,
        b_key,
        b_value,
        k_cache[:, 0],
        v_cache[:, 0],
        w_query,
        w_key.T,
        w_value.T,
        w_out,
        w_head,
    )
    targets = rep_pos * serve + jnp.arange(serve, dtype=jnp.int32)
    equal = dest_flat[None, :] == targets[:, None]
    lens = jnp.sum(jnp.where(equal, lengths[None, :] + 1, 0), axis=1) - 1
    valid = lens >= 0
    keys_served = write_newest(got_k, new_k, lens, valid, part)
    values_served = write_newest(got_v, new_v, lens, valid, part)
    share = serve // n_tp
    wanted = (rep_pos * n_tp + tp_pos) * share + jnp.arange(share, dtype=jnp.int32)
    here = dest_flat[None, :] == wanted[:, None]
    chosen = jnp.sum(jnp.where(here[None], best[:2, None, :], 0.0), axis=2)
    top_logit, final_norm = chosen[0], chosen[1]
    return (final_norm, top_logit, keys_served[:, None], values_served[:, None])


def solution(mesh):
    in_specs = (
        P("rep", None),
        P("rep", "tp", None, None),
        P("rep", "tp", None, None),
        P(),
        P(),
        P(None, "tp"),
        P("tp"),
        P(None, "tp"),
        P("tp"),
        P(None, "tp"),
        P("tp"),
        P("tp", None),
        P(),
        P(),
        P(("rep", "tp"), None),
    )
    out_specs = (
        P(("rep", "tp")),
        P(("rep", "tp")),
        P("rep", "tp", None, None),
        P("rep", "tp", None, None),
    )
    small = mesh.shape["rep"] == 8 and mesh.shape["tp"] == 4
    return jax.shard_map(
        fast_device if small else per_device, mesh=mesh, in_specs=in_specs, out_specs=out_specs, check_vma=False
    )
```
